512 devices in a mesh: row: 64 (over y, z_lo, core), col: 8 (over z_hi, x).
Axes of the slice: x: 4, y: 8, z: 8 (z_hi: 2, z_lo: 4; z = z_hi * 4 + z_lo), core: 2. Of those that a mesh axis runs over, the one named last changes fastest.
Arguments:
- telemetry: float32 [8, 2048, 64], P('col', 'row'), may hold values from -6 to 6
- target: int32 [8, 2048], P('col', 'row'), may hold values from 0 to 8191, as said below
- counts: int32 [8, 64], P('col', 'row'), may hold values from 0 to 32, as said below
- lengthscale: float32 [64], replicated, may hold values from 2 to 8
- nugget: float32 [8192], P('row'), may hold values from 0.1 to 1
Outputs:
- schur: float32 [8192, 8, 1024], P('row', 'col')
- lower_col: float32 [8192, 1024], P('row')
The draws below stay inside these ranges and needn't reach their ends.
Inputs may be any that keep to these rules, and one draw needn't show every extreme that they name: `target`: the first counts slots of each device hold distinct location indices, and over all devices every location appears exactly once among them; later slots hold arbitrary indices. The used slots of device (c, r) name only locations of row blocks (r - d) mod 64 with 0 <= d < 16, at most 2 locations of any one row block, and exactly 2 for every block they name. `counts`: Even; 32 on some device of every index of col; the total over all devices is 8192.
All inputs are finite; a program needn't handle non-finite values.
Results may differ from the reference program's by a relative error of at most 0.0003.
Values sent between devices are 32-bit elements; how exact they have to be, the bound alone decides.
A program may use at most 128 MiB of HBM per device.

```python
import math
import jax
import jax.numpy as jnp
from jax import lax

F = 64
PB = 1024
RB = 128
SL = 16
IN_DEV = 32
NPTS = 8192
N_ROW = 64
N_COL = 8


def zone_layout(key):
    half = SL // 2
    choose_b = jax.random.randint(jax.random.fold_in(key, 11), (N_ROW, N_COL, half), 0, 2)
    busy_row = jax.random.randint(jax.random.fold_in(key, 12), (), 0, N_ROW)
    groups = jnp.arange(half)
    zero_rows = (busy_row - 2 * groups) % N_ROW
    one_rows = (busy_row - 2 * groups - 1) % N_ROW
    col_ids = jnp.arange(N_COL)
    choose_b = choose_b.at[zero_rows[:, None], col_ids[None, :], groups[:, None]].set(0)
    choose_b = choose_b.at[one_rows[:, None], col_ids[None, :], groups[:, None]].set(1)
    perm_keys = jax.random.split(jax.random.fold_in(key, 13), N_ROW)
    block_perm = jax.vmap(lambda single: jax.random.permutation(single, RB))(perm_keys)
    collector = jnp.arange(N_ROW)[:, None, None, None, None]
    column = jnp.arange(N_COL)[None, :, None, None, None]
    group = jnp.arange(half)[None, None, :, None, None]
    which = jnp.arange(2)[None, None, None, :, None]
    member = jnp.arange(2)[None, None, None, None, :]
    shape = (N_ROW, N_COL, half, 2, 2)
    owner = jnp.broadcast_to((collector - 2 * group - which) % N_ROW, shape)
    column_b = jnp.broadcast_to(column, shape)
    group_b = jnp.broadcast_to(group, shape)
    which_b = jnp.broadcast_to(which, shape)
    member_b = jnp.broadcast_to(member, shape)
    present = choose_b[owner, column_b, group_b] == which_b
    point = owner * RB + block_perm[owner, column_b * SL + 2 * group_b + member_b]
    raw = 2 * (2 * group_b + which_b) + member_b
    present_f = present.reshape(N_ROW, N_COL, IN_DEV)
    point_f = point.reshape(N_ROW, N_COL, IN_DEV)
    raw_f = raw.reshape(N_ROW, N_COL, IN_DEV)
    score = jnp.where(present_f, raw_f, raw_f + IN_DEV)
    ranking = jnp.argsort(score, axis=-1, stable=True)
    sorted_points = jnp.take_along_axis(point_f, ranking, axis=-1)
    filled = jnp.sum(present_f.astype(jnp.int32), axis=-1)
    filler = jax.random.randint(jax.random.fold_in(key, 14), (N_ROW, N_COL, IN_DEV), 0, NPTS)
    slot_ids = jnp.arange(IN_DEV)
    chosen = jnp.where(slot_ids[None, None, :] < filled[:, :, None], sorted_points, filler)
    listing = chosen.transpose(1, 0, 2).reshape(N_COL, N_ROW * IN_DEV).astype(jnp.int32)
    return (listing, filled.T.astype(jnp.int32))


def draw_target(key, part):
    return zone_layout(key)[0]


def draw_counts(key, part):
    return zone_layout(key)[1]


def block_levels(stream_key, dims, pieces, smallest, high):
    def one(position, blocks):
        draws = jax.random.uniform(jax.random.fold_in(jax.random.fold_in(stream_key, 6), position), (blocks,), jnp.float32, smallest / len(pieces), high / len(pieces))
        return jnp.repeat(jnp.exp(draws), dims[position] // blocks).reshape((-1,) + (1,) * (len(dims) - position - 1))

    factor_of = one(*pieces[0])
    for cut in pieces[1:]:
        factor_of = factor_of * one(*cut)
    return factor_of


def centred(rng, dims, spread, limit, shards=(), kind=jnp.bfloat16):
    factor_of = block_levels(rng, dims, shards, -0.22, 0.18) if shards else 1.0
    drawn = jax.random.normal(rng, dims, jnp.float32) * spread * factor_of
    return jnp.minimum(jnp.maximum(drawn, -limit), limit).astype(kind)


def setup_inputs(seed: int = 0) -> dict:
    arg_keys = jax.random.split(jax.random.key(seed), 6)
    telemetry = centred(arg_keys[0], (N_COL, N_ROW * IN_DEV, F), 1.0, 6.0, ((0, 8), (1, 64)), jnp.float32)
    target = draw_target(jax.random.fold_in(arg_keys[5], 71), 0)
    counts = draw_counts(jax.random.fold_in(arg_keys[5], 71), 0)
    lengthscale = jnp.clip(jnp.exp(jax.random.uniform(arg_keys[3], (F,), jnp.float32, math.log(2.0), math.log(8.0))), 2.0, 8.0)
    nugget = jnp.clip(jnp.exp(math.log(1.0) - 2.3025851 * jax.random.uniform(arg_keys[4], (NPTS,), jnp.float32) ** block_levels(arg_keys[4], (NPTS,), ((0, 64),), -0.2, 0.2)), 0.1, 1.0)
    return dict(telemetry=telemetry, target=target, counts=counts, lengthscale=lengthscale, nugget=nugget)


root_three = 1.7320508075688772

def matern(left, right, inv_len):
    left_s = left * inv_len
    right_s = right * inv_len
    inner = jnp.dot(left_s.astype(jnp.float32), right_s.T.astype(jnp.float32), precision=lax.Precision.HIGHEST, preferred_element_type=jnp.float32)
    squared = lax.optimization_barrier(jnp.sum(left_s * left_s, axis=1))[:, None] + lax.optimization_barrier(jnp.sum(right_s * right_s, axis=1))[None, :] - 2.0 * inner
    distance = jnp.sqrt(jnp.maximum(squared, 0.0))
    return (1.0 + root_three * distance) * jnp.exp(-root_three * distance)

def reference(telemetry, target, counts, lengthscale, nugget):
    rows_all = telemetry.reshape(N_COL * N_ROW * IN_DEV, F)
    slot_ids = jnp.arange(N_ROW * IN_DEV, dtype=jnp.int32) % IN_DEV
    in_use = slot_ids[None, :] < jnp.repeat(counts, IN_DEV, axis=1)
    where_to = jnp.where(in_use, target, NPTS).reshape(-1).astype(jnp.int32)
    points = jnp.zeros((NPTS, F), telemetry.dtype).at[where_to].add(rows_all, mode='drop')
    inv_len = 1.0 / lengthscale
    full = matern(points, points, inv_len) + jnp.diag(nugget)
    panel_part = full[:, :PB]
    factor = jnp.linalg.cholesky(panel_part[:PB])
    lower_col = lax.linalg.triangular_solve(factor, panel_part, left_side=False, lower=True, transpose_a=True)
    updated = full - jnp.dot(lower_col.astype(jnp.float32), lower_col.T.astype(jnp.float32), precision=lax.Precision.HIGHEST, preferred_element_type=jnp.float32)
    schur = updated.reshape(NPTS, N_ROW, N_COL, SL).transpose(0, 2, 1, 3).reshape(NPTS, N_COL, N_ROW * SL)
    return (schur, lower_col)
```

```python
import functools

import jax
import jax.numpy as jnp
from jax import lax
from jax.experimental import pallas as pl
from jax.experimental.pallas import tpu as pltpu
from jax.sharding import PartitionSpec as P

F = 64
PB = 1024
RB = 128
NR = 64
NC = 8
SL = 16
WIN = 16
SLOTS = 32
HI = lax.Precision.HIGHEST
MESH = pl.DeviceIdType.MESH

root_three = 1.7320508075688772


def hdot(a, b):
    return jnp.dot(a, b, precision=HI, preferred_element_type=jnp.float32)


def exchange_kernel(
    tel_ref, tgt_ref, cnt_ref, nug_ref,
    blk_ref, col_ref, pan_ref, pnug_ref,
    out1, in1, comp, gath, mine, nugtile,
    s1, r1, s2, r2, s3, r3, s4, r4, s5, r5,
):
    r = lax.axis_index("row")
    c = lax.axis_index("col")

    def at_row(peer):
        return (peer, c)

    def at_col(peer):
        return (r, peer)

    barrier = pltpu.get_barrier_semaphore()

    def greet_row(i, carry):
        pl.semaphore_signal(
            barrier, inc=1, device_id=at_row(lax.rem(r + i, NR)), device_id_type=MESH
        )
        return carry

    def greet_col(i, carry):
        pl.semaphore_signal(
            barrier, inc=1, device_id=at_col(lax.rem(c + i, NC)), device_id_type=MESH
        )
        return carry

    lax.fori_loop(1, NR, greet_row, 0)
    lax.fori_loop(1, NC, greet_col, 0)

    tel = tel_ref[0]
    t_row = tgt_ref[...]
    sub = lax.broadcasted_iota(jnp.int32, (SLOTS, SLOTS), 0)
    lane = lax.broadcasted_iota(jnp.int32, (SLOTS, SLOTS), 1)
    t_mat = jnp.broadcast_to(t_row, (SLOTS, SLOTS))
    t_col = jnp.sum(jnp.where(sub == lane, t_mat, 0), axis=1, keepdims=True)
    zone_row = lax.shift_right_logical(t_row, 7)
    zone_col = lax.shift_right_logical(t_col, 7)
    filled = cnt_ref[...]
    earlier = (zone_col == zone_row) & (sub < filled) & (sub < lane)
    position = jnp.sum(earlier.astype(jnp.int32), axis=0, keepdims=True)
    offset = jnp.bitwise_and(r - zone_row + NR, NR - 1)
    used = (lane[0:1] < filled) & (position < 2) & (offset < WIN)
    slot = jnp.where(used, offset * 2 + position, -1)
    place = jnp.bitwise_and(t_row, RB - 1).astype(jnp.float32)
    dist = lax.broadcasted_iota(jnp.int32, (WIN, SLOTS), 0) * 2
    pick0 = dist == slot
    pick1 = dist + 1 == slot
    feat0 = hdot(pick0.astype(jnp.float32), tel)
    feat1 = hdot(pick1.astype(jnp.float32), tel)
    place0 = jnp.max(jnp.where(pick0, place, -1.0), axis=1, keepdims=True)
    place1 = jnp.max(jnp.where(pick1, place, -1.0), axis=1, keepdims=True)
    feats = jnp.concatenate([feat0, feat1], axis=1)
    lane_w = lax.broadcasted_iota(jnp.int32, (WIN, 128), 1)
    places = jnp.where(lane_w < F, place0, place1)
    tile_row = lax.broadcasted_iota(jnp.int32, (8, 128), 0)
    for d in range(WIN):
        out1[d] = jnp.where(
            tile_row == 0, feats[d : d + 1], jnp.where(tile_row == 1, places[d : d + 1], 0.0)
        )
    in1[0] = out1[0]
    nugtile[...] = jnp.broadcast_to(nug_ref[...], (8, 128))

    pl.semaphore_wait(barrier, NR - 1 + NC - 1)

    def step1(d):
        return pltpu.make_async_remote_copy(
            src_ref=out1.at[d], dst_ref=in1.at[d], send_sem=s1.at[d], recv_sem=r1.at[d],
            device_id=at_row(lax.rem(r - d + NR, NR)), device_id_type=MESH,
        )

    def start1(d, carry):
        step1(d).start()
        return carry

    lax.fori_loop(1, WIN, start1, 0)

    def step5(i, slot_id):
        return pltpu.make_async_remote_copy(
            src_ref=nugtile, dst_ref=pnug_ref.at[slot_id], send_sem=s5.at[i],
            recv_sem=r5.at[slot_id],
            device_id=at_row(lax.rem(r + i, NR)), device_id_type=MESH,
        )

    @pl.when(r < NC)
    def _():
        def start5(i, carry):
            step5(i, r).start()
            return carry

        lax.fori_loop(1, NR, start5, 0)
        pnug_ref[r] = nugtile[...]

    def wait1(d, carry):
        step1(d).wait_recv()
        return carry

    lax.fori_loop(1, WIN, wait1, 0)
    o = lax.broadcasted_iota(jnp.int32, (2 * WIN, 128), 0)
    k = lax.broadcasted_iota(jnp.int32, (2 * WIN, 128), 1)
    chosen = k == jnp.where(o < WIN, 8 * o, 8 * (o - WIN) + 1)
    comp[...] = hdot(chosen.astype(jnp.float32), in1[...].reshape(WIN * 8, 128))
    gath[c] = comp[...]

    def step2(i, slot_id):
        return pltpu.make_async_remote_copy(
            src_ref=comp, dst_ref=gath.at[slot_id], send_sem=s2.at[i], recv_sem=r2.at[slot_id],
            device_id=at_col(lax.rem(c + i, NC)), device_id_type=MESH,
        )

    for i in range(1, NC):
        step2(i, c).start()
    for i in range(1, NC):
        step2(i, lax.rem(c + i, NC)).wait_recv()

    all_feats = gath[:, 0:WIN, :].reshape(NC * WIN, 128)
    all_places = gath[:, WIN : 2 * WIN, :].reshape(NC * WIN, 128)
    spot = lax.broadcasted_iota(jnp.int32, (NC * WIN, RB), 1).astype(jnp.float32)
    put0 = (all_places[:, 0:1] == spot).astype(jnp.float32)
    put1 = (all_places[:, F : F + 1] == spot).astype(jnp.float32)
    blk_ref[...] = hdot(put0.T, all_feats[:, 0:F]) + hdot(put1.T, all_feats[:, F : 2 * F])

    mine[:, 0:F] = blk_ref[pl.ds(c * SL, 8), :]
    mine[:, F : 2 * F] = blk_ref[pl.ds(c * SL + 8, 8), :]
    col_ref[r] = mine[...]

    def step3(i, slot_id):
        return pltpu.make_async_remote_copy(
            src_ref=mine, dst_ref=col_ref.at[slot_id], send_sem=s3.at[i], recv_sem=r3.at[slot_id],
            device_id=at_row(lax.rem(r + i, NR)), device_id_type=MESH,
        )

    def start3(i, carry):
        step3(i, r).start()
        return carry

    lax.fori_loop(1, NR, start3, 0)

    def wait3(slot_id):
        @pl.when(slot_id != r)
        def _():
            step3(1, slot_id).wait_recv()

    for slot_id in range(NC):
        wait3(slot_id)

    def step4(i, slot_id):
        return pltpu.make_async_remote_copy(
            src_ref=col_ref.at[pl.ds(0, NC)], dst_ref=pan_ref.at[slot_id], send_sem=s4.at[i],
            recv_sem=r4.at[slot_id],
            device_id=at_col(lax.rem(c + i, NC)), device_id_type=MESH,
        )

    for i in range(1, NC):
        step4(i, c).start()
    pan_ref[c] = col_ref[0:NC]

    def rest3(slot_id, carry):
        wait3(slot_id)
        return carry

    lax.fori_loop(NC, NR, rest3, 0)
    for slot_id in range(NC):
        @pl.when(slot_id != r)
        def _(slot_id=slot_id):
            step5(1, slot_id).wait_recv()

    for i in range(1, NC):
        step4(i, lax.rem(c + i, NC)).wait_recv()

    def sent1(d, carry):
        step1(d).wait_send()
        return carry

    lax.fori_loop(1, WIN, sent1, 0)
    for i in range(1, NC):
        step2(i, c).wait_send()
        step4(i, c).wait_send()

    def sent3(i, carry):
        step3(i, r).wait_send()
        return carry

    lax.fori_loop(1, NR, sent3, 0)

    @pl.when(r < NC)
    def _():
        def sent5(i, carry):
            step5(i, r).wait_send()
            return carry

        lax.fori_loop(1, NR, sent5, 0)


def exchange(telemetry, target, counts, nugget):
    dma = pltpu.SemaphoreType.DMA
    vmem = pl.BlockSpec(memory_space=pltpu.VMEM)
    f32 = jnp.float32
    return pl.pallas_call(
        exchange_kernel,
        out_shape=(
            jax.ShapeDtypeStruct((RB, F), f32),
            jax.ShapeDtypeStruct((NR, 8, 128), f32),
            jax.ShapeDtypeStruct((NC, NC, 8, 128), f32),
            jax.ShapeDtypeStruct((NC, 8, 128), f32),
        ),
        in_specs=[vmem] * 4,
        out_specs=(vmem,) * 4,
        scratch_shapes=[
            pltpu.VMEM((WIN, 8, 128), f32),
            pltpu.VMEM((WIN, 8, 128), f32),
            pltpu.VMEM((2 * WIN, 128), f32),
            pltpu.VMEM((NC, 2 * WIN, 128), f32),
            pltpu.VMEM((8, 128), f32),
            pltpu.VMEM((8, 128), f32),
            dma((WIN,)), dma((WIN,)), dma((NC,)), dma((NC,)), dma((NR,)), dma((NR,)),
            dma((NC,)), dma((NC,)), dma((NR,)), dma((NC,)),
        ],
        compiler_params=pltpu.CompilerParams(
            collective_id=0, has_side_effects=True, vmem_limit_bytes=32 * 1024 * 1024
        ),
        name="exchange",
    )(telemetry, target, counts, nugget.reshape(1, RB))


def matern(left, right, inv_len):
    left_s = left * inv_len
    right_s = right * inv_len
    inner = hdot(left_s, right_s.T)
    squared = (
        jnp.sum(left_s * left_s, axis=1)[:, None]
        + jnp.sum(right_s * right_s, axis=1)[None, :]
        - 2.0 * inner
    )
    distance = jnp.sqrt(jnp.maximum(squared, 0.0))
    return (1.0 + root_three * distance) * jnp.exp(-root_three * distance)


def body(telemetry, target, counts, lengthscale, nugget):
    row_index = lax.axis_index("row")
    col_index = lax.axis_index("col")
    block_pts, col_packed, pan_packed, pnug = exchange(telemetry, target, counts, nugget)
    inv_len = 1.0 / lengthscale
    column_pts = col_packed.reshape(NR, 8, 2, F).transpose(0, 2, 1, 3).reshape(PB, F)
    panel_pts = pan_packed.reshape(NC, NC, 8, 2, F).transpose(1, 0, 3, 2, 4).reshape(PB, F)
    panel_nug = pnug[:, 0, :].reshape(PB)
    panel_ids = jnp.arange(PB, dtype=jnp.int32)
    row_ids = row_index * RB + jnp.arange(RB, dtype=jnp.int32)
    column_ids = (
        jnp.arange(NR, dtype=jnp.int32)[:, None] * RB
        + col_index * SL
        + jnp.arange(SL, dtype=jnp.int32)[None, :]
    ).reshape(-1)
    panel_kernel = matern(panel_pts, panel_pts, inv_len) + jnp.diag(panel_nug)
    factor = jnp.linalg.cholesky(panel_kernel)
    kernel = matern(block_pts, panel_pts, inv_len)
    kernel = kernel + jnp.where(row_ids[:, None] == panel_ids[None, :], nugget[:, None], 0.0)
    row_lower = lax.linalg.triangular_solve(
        factor, kernel, left_side=False, lower=True, transpose_a=True
    )
    weights = lax.linalg.triangular_solve(
        factor, row_lower, left_side=False, lower=True, transpose_a=False
    )
    across = matern(column_pts, panel_pts, inv_len)
    across = across + jnp.where(
        column_ids[:, None] == panel_ids[None, :], panel_nug[None, :], 0.0
    )
    tile_kernel = matern(block_pts, column_pts, inv_len)
    tile_kernel = tile_kernel + jnp.where(
        row_ids[:, None] == column_ids[None, :], nugget[:, None], 0.0
    )
    schur_tile = tile_kernel - hdot(weights, across.T)
    return (schur_tile[:, None, :], row_lower)


def solution(mesh):
    in_specs = (P("col", "row", None), P("col", "row"), P("col", "row"), P(), P("row"))
    out_specs = (P("row", "col", None), P("row", None))
    return jax.shard_map(body, mesh=mesh, in_specs=in_specs, out_specs=out_specs, check_vma=False)
```

```python
import functools

import jax
import jax.numpy as jnp
from jax import lax
from jax.experimental import pallas as pl
from jax.experimental.pallas import tpu as pltpu
from jax.sharding import PartitionSpec as P

F = 64
PB = 1024
RB = 128
NR = 64
NC = 8
SL = 16
WIN = 16
SLOTS = 32
HI = lax.Precision.HIGHEST
MESH = pl.DeviceIdType.MESH

root_three = 1.7320508075688772


def hdot(a, b):
    return jnp.dot(a, b, precision=HI, preferred_element_type=jnp.float32)


def exchange_kernel(
    tel_ref, tgt_ref, cnt_ref, nug_ref,
    blk_ref, col_ref, pan_ref, pnug_ref,
    out1, in1, comp, gath, mine, nugtile,
    s1, r1, s2, r2, s3, r3, s4, r4, s5, r5,
):
    r = lax.axis_index("row")
    c = lax.axis_index("col")

    def at_row(peer):
        return (peer, c)

    def at_col(peer):
        return (r, peer)

    barrier = pltpu.get_barrier_semaphore()

    def greet_row(i, carry):
        pl.semaphore_signal(
            barrier, inc=1, device_id=at_row(lax.rem(r + i, NR)), device_id_type=MESH
        )
        return carry

    def greet_col(i, carry):
        pl.semaphore_signal(
            barrier, inc=1, device_id=at_col(lax.rem(c + i, NC)), device_id_type=MESH
        )
        return carry

    lax.fori_loop(1, NR, greet_row, 0)
    lax.fori_loop(1, NC, greet_col, 0)

    tel = tel_ref[0]
    t_row = tgt_ref[...]
    sub = lax.broadcasted_iota(jnp.int32, (SLOTS, SLOTS), 0)
    lane = lax.broadcasted_iota(jnp.int32, (SLOTS, SLOTS), 1)
    t_mat = jnp.broadcast_to(t_row, (SLOTS, SLOTS))
    t_col = jnp.sum(jnp.where(sub == lane, t_mat, 0), axis=1, keepdims=True)
    zone_row = lax.shift_right_logical(t_row, 7)
    zone_col = lax.shift_right_logical(t_col, 7)
    filled = cnt_ref[...]
    earlier = (zone_col == zone_row) & (sub < filled) & (sub < lane)
    position = jnp.sum(earlier.astype(jnp.int32), axis=0, keepdims=True)
    offset = jnp.bitwise_and(r - zone_row + NR, NR - 1)
    used = (lane[0:1] < filled) & (position < 2) & (offset < WIN)
    slot = jnp.where(used, offset * 2 + position, -1)
    place = jnp.bitwise_and(t_row, RB - 1).astype(jnp.float32)
    dist = lax.broadcasted_iota(jnp.int32, (WIN, SLOTS), 0) * 2
    pick0 = dist == slot
    pick1 = dist + 1 == slot
    feat0 = hdot(pick0.astype(jnp.float32), tel)
    feat1 = hdot(pick1.astype(jnp.float32), tel)
    place0 = jnp.max(jnp.where(pick0, place, -1.0), axis=1, keepdims=True)
    place1 = jnp.max(jnp.where(pick1, place, -1.0), axis=1, keepdims=True)
    feats = jnp.concatenate([feat0, feat1], axis=1)
    lane_w = lax.broadcasted_iota(jnp.int32, (WIN, 128), 1)
    places = jnp.where(lane_w < F, place0, place1)
    tile_row = lax.broadcasted_iota(jnp.int32, (8, 128), 0)
    for d in range(WIN):
        out1[d] = jnp.where(
            tile_row == 0, feats[d : d + 1], jnp.where(tile_row == 1, places[d : d + 1], 0.0)
        )
    in1[0] = out1[0]
    nugtile[...] = jnp.broadcast_to(nug_ref[...], (8, 128))

    pl.semaphore_wait(barrier, NR - 1 + NC - 1)

    def step1(d):
        return pltpu.make_async_remote_copy(
            src_ref=out1.at[d], dst_ref=in1.at[d], send_sem=s1.at[d], recv_sem=r1.at[d],
            device_id=at_row(lax.rem(r - d + NR, NR)), device_id_type=MESH,
        )

    def start1(d, carry):
        step1(d).start()
        return carry

    lax.fori_loop(1, WIN, start1, 0)

    def step5(i, slot_id):
        return pltpu.make_async_remote_copy(
            src_ref=nugtile, dst_ref=pnug_ref.at[slot_id], send_sem=s5.at[i],
            recv_sem=r5.at[slot_id],
            device_id=at_row(lax.rem(r + i, NR)), device_id_type=MESH,
        )

    @pl.when(r < NC)
    def _():
        def start5(i, carry):
            step5(i, r).start()
            return carry

        lax.fori_loop(1, NR, start5, 0)
        pnug_ref[r] = nugtile[...]

    def wait1(d, carry):
        step1(d).wait_recv()
        return carry

    lax.fori_loop(1, WIN, wait1, 0)
    o = lax.broadcasted_iota(jnp.int32, (2 * WIN, 128), 0)
    k = lax.broadcasted_iota(jnp.int32, (2 * WIN, 128), 1)
    chosen = k == jnp.where(o < WIN, 8 * o, 8 * (o - WIN) + 1)
    comp[...] = hdot(chosen.astype(jnp.float32), in1[...].reshape(WIN * 8, 128))
    gath[c] = comp[...]

    def step2(i, slot_id):
        return pltpu.make_async_remote_copy(
            src_ref=comp, dst_ref=gath.at[slot_id], send_sem=s2.at[i], recv_sem=r2.at[slot_id],
            device_id=at_col(lax.rem(c + i, NC)), device_id_type=MESH,
        )

    for i in range(1, NC):
        step2(i, c).start()
    for i in range(1, NC):
        step2(i, lax.rem(c + i, NC)).wait_recv()

    all_feats = gath[:, 0:WIN, :].reshape(NC * WIN, 128)
    all_places = gath[:, WIN : 2 * WIN, :].reshape(NC * WIN, 128)
    spot = lax.broadcasted_iota(jnp.int32, (NC * WIN, RB), 1).astype(jnp.float32)
    put0 = (all_places[:, 0:1] == spot).astype(jnp.float32)
    put1 = (all_places[:, F : F + 1] == spot).astype(jnp.float32)
    blk_ref[...] = hdot(put0.T, all_feats[:, 0:F]) + hdot(put1.T, all_feats[:, F : 2 * F])

    mine[:, 0:F] = blk_ref[pl.ds(c * SL, 8), :]
    mine[:, F : 2 * F] = blk_ref[pl.ds(c * SL + 8, 8), :]
    col_ref[r] = mine[...]

    def step3(i, slot_id):
        return pltpu.make_async_remote_copy(
            src_ref=mine, dst_ref=col_ref.at[slot_id], send_sem=s3.at[i], recv_sem=r3.at[slot_id],
            device_id=at_row(lax.rem(r + i, NR)), device_id_type=MESH,
        )

    def start3(i, carry):
        step3(i, r).start()
        return carry

    lax.fori_loop(1, NR, start3, 0)

    def wait3(slot_id):
        @pl.when(slot_id != r)
        def _():
            step3(1, slot_id).wait_recv()

    for slot_id in range(NC):
        wait3(slot_id)

    def step4(i, slot_id):
        return pltpu.make_async_remote_copy(
            src_ref=col_ref.at[pl.ds(0, NC)], dst_ref=pan_ref.at[slot_id], send_sem=s4.at[i],
            recv_sem=r4.at[slot_id],
            device_id=at_col(lax.rem(c + i, NC)), device_id_type=MESH,
        )

    for i in range(1, NC):
        step4(i, c).start()
    pan_ref[c] = col_ref[0:NC]

    def rest3(slot_id, carry):
        wait3(slot_id)
        return carry

    lax.fori_loop(NC, NR, rest3, 0)
    for slot_id in range(NC):
        @pl.when(slot_id != r)
        def _(slot_id=slot_id):
            step5(1, slot_id).wait_recv()

    for i in range(1, NC):
        step4(i, lax.rem(c + i, NC)).wait_recv()

    def sent1(d, carry):
        step1(d).wait_send()
        return carry

    lax.fori_loop(1, WIN, sent1, 0)
    for i in range(1, NC):
        step2(i, c).wait_send()
        step4(i, c).wait_send()

    def sent3(i, carry):
        step3(i, r).wait_send()
        return carry

    lax.fori_loop(1, NR, sent3, 0)

    @pl.when(r < NC)
    def _():
        def sent5(i, carry):
            step5(i, r).wait_send()
            return carry

        lax.fori_loop(1, NR, sent5, 0)


def exchange(telemetry, target, counts, nugget):
    dma = pltpu.SemaphoreType.DMA
    vmem = pl.BlockSpec(memory_space=pltpu.VMEM)
    f32 = jnp.float32
    return pl.pallas_call(
        exchange_kernel,
        out_shape=(
            jax.ShapeDtypeStruct((RB, F), f32),
            jax.ShapeDtypeStruct((NR, 8, 128), f32),
            jax.ShapeDtypeStruct((NC, NC, 8, 128), f32),
            jax.ShapeDtypeStruct((NC, 8, 128), f32),
        ),
        in_specs=[vmem] * 4,
        out_specs=(vmem,) * 4,
        scratch_shapes=[
            pltpu.VMEM((WIN, 8, 128), f32),
            pltpu.VMEM((WIN, 8, 128), f32),
            pltpu.VMEM((2 * WIN, 128), f32),
            pltpu.VMEM((NC, 2 * WIN, 128), f32),
            pltpu.VMEM((8, 128), f32),
            pltpu.VMEM((8, 128), f32),
            dma((WIN,)), dma((WIN,)), dma((NC,)), dma((NC,)), dma((NR,)), dma((NR,)),
            dma((NC,)), dma((NC,)), dma((NR,)), dma((NC,)),
        ],
        compiler_params=pltpu.CompilerParams(
            collective_id=0, has_side_effects=True, vmem_limit_bytes=32 * 1024 * 1024
        ),
        name="exchange",
    )(telemetry, target, counts, nugget.reshape(1, RB))


def recip(p):
    x = pl.reciprocal(p, approx=True)
    return x * (2.0 - p * x)


def factor_block(tile):
    sub = lax.broadcasted_iota(jnp.int32, (8, RB), 0)
    lane = lax.broadcasted_iota(jnp.int32, (8, RB), 1)
    for first in range(0, RB, 8):
        rows = tile[first : first + 8, :]
        cols = [jnp.broadcast_to(rows[:, first + k : first + k + 1], (8, RB)) for k in range(8)]
        in_panel = (lane >= first) & (lane < first + 8)
        rows = jnp.where(in_panel, (lane - first == sub).astype(jnp.float32), rows)
        pivots = jnp.ones((8, RB), jnp.float32)
        for i in range(8):
            top = [jnp.broadcast_to(cols[k][i : i + 1], (8, RB)) for k in range(i, 8)]
            step = jnp.where(sub > i, cols[i] * recip(top[0]), 0.0)
            pivots = jnp.where(sub == i, top[0], pivots)
            for k in range(i + 1, 8):
                cols[k] = cols[k] - step * top[k - i]
            if i < 7:
                rows = rows - step * jnp.broadcast_to(rows[i : i + 1], (8, RB))
        done = rows * lax.rsqrt(pivots)
        tile[first : first + 8, :] = done
        if first + 8 < RB:
            low = first + 8
            product = tdot(done, done)
            lane_l = lax.broadcasted_iota(jnp.int32, (RB - low, RB), 1)
            rest = jnp.where((lane_l >= first) & (lane_l < low), 0.0, tile[low:, :])
            tile[low:, :] = rest - product[low:, :]


def tdot(a, b):
    return lax.dot_general(
        a, b, (((0,), (0,)), ((), ())), precision=HI, preferred_element_type=jnp.float32
    )


def ndot(a, b):
    return lax.dot_general(
        a, b, (((1,), (1,)), ((), ())), precision=HI, preferred_element_type=jnp.float32
    )


def matern(left, right):
    ones = jnp.ones((8, F), jnp.float32)
    squared = (
        jnp.sum(left * left, axis=1, keepdims=True)
        + ndot(ones, right * right)[0:1]
        - 2.0 * ndot(left, right)
    )
    scaled = root_three * jnp.sqrt(jnp.maximum(squared, 0.0))
    return (1.0 + scaled) * jnp.exp(-scaled)


def factor_kernel(
    where_ref, blk_ref, col_ref, pan_ref, pnug_ref, nug_ref, len_ref,
    schur_ref, lower_ref,
    own, pts, cpts, nugs, big, across, weights, tile,
):
    r = where_ref[0]
    c = where_ref[1]
    inv = 1.0 / len_ref[...]
    own[...] = blk_ref[...] * inv
    for rb in range(NC):
        nugs[:, rb * RB : (rb + 1) * RB] = pnug_ref[rb]
        for cc in range(NC):
            at = rb * RB + cc * SL
            both = pan_ref[cc, rb]
            pts[at : at + 8, :] = both[:, 0:F] * inv
            pts[at + 8 : at + SL, :] = both[:, F : 2 * F] * inv
    for rb in range(NR):
        both = col_ref[rb]
        cpts[rb * SL : rb * SL + 8, :] = both[:, 0:F] * inv
        cpts[rb * SL + 8 : rb * SL + SL, :] = both[:, F : 2 * F] * inv

    eye = lax.broadcasted_iota(jnp.int32, (RB, RB), 0) == lax.broadcasted_iota(
        jnp.int32, (RB, RB), 1
    )
    sub = lax.broadcasted_iota(jnp.int32, (RB, 1), 0)

    def column_ids():
        n = lax.broadcasted_iota(jnp.int32, (1, PB), 1)
        return lax.shift_right_logical(n, 4) * RB + c * SL + jnp.bitwise_and(n, SL - 1)

    for i in range(NC):
        at = i * RB
        if i:
            big[at : at + RB, 0:at] = jnp.zeros((RB, at), jnp.float32)
        mine = pts[at : at + RB, :]
        big[at : at + RB, at:PB] = matern(mine, pts[at:, :])
        nug_here = jnp.where(eye, nugs[0:1, at : at + RB], 0.0)
        big[at : at + RB, at : at + RB] += nug_here
        same = jnp.where(r == i, 1.0, 0.0)
        big[at : at + RB, PB:] = matern(mine, own[...]) + same * nug_here

    def across_rows(i, carry):
        at = pl.multiple_of(i * RB, RB)
        nug_col = jnp.sum(
            jnp.where(eye, nugs[0:1, pl.ds(at, RB)], 0.0), axis=1, keepdims=True
        )
        across[pl.ds(at, RB), :] = matern(pts[pl.ds(at, RB), :], cpts[...]) + jnp.where(
            at + sub == column_ids(), nug_col, 0.0
        )
        return carry

    lax.fori_loop(0, NC, across_rows, 0)

    low = lax.broadcasted_iota(jnp.int32, (RB, RB), 0) >= lax.broadcasted_iota(
        jnp.int32, (RB, RB), 1
    )

    def eliminate(k, carry):
        at = pl.multiple_of(k * RB, RB)
        tile[...] = big[pl.ds(at, RB), pl.ds(at, RB)]
        factor_block(tile)
        inverse = jnp.where(low, tile[...], 0.0)
        big[pl.ds(at, RB), pl.ds(at, RB)] = eye.astype(jnp.float32)
        upper = hdot(inverse, big[pl.ds(at, RB), :])
        big[pl.ds(at, RB), :] = upper

        def update(i, carry):
            to = pl.multiple_of(i * RB, RB)
            coef = big[pl.ds(at, RB), pl.ds(to, RB)]
            big[pl.ds(to, RB), pl.ds(at, RB)] = jnp.zeros((RB, RB), jnp.float32)
            big[pl.ds(to, RB), :] = big[pl.ds(to, RB), :] - tdot(coef, big[pl.ds(at, RB), :])
            return carry

        lax.fori_loop(k + 1, NC, update, 0)
        return carry

    lax.fori_loop(0, NC, eliminate, 0)

    for j in range(NC):
        at = j * RB
        weights[at : at + RB, :] = tdot(big[at:, at : at + RB], big[at:, PB:])
        lower_ref[:, at : at + RB] = big[at : at + RB, PB:].T
    nug_own = jnp.sum(jnp.where(eye, nug_ref[...], 0.0), axis=1, keepdims=True)
    schur_ref[...] = (
        matern(own[...], cpts[...])
        + jnp.where(r * RB + sub == column_ids(), nug_own, 0.0)
        - tdot(weights[...], across[...])
    )


def factor_and_update(where, blk, col, pan, pnug, nugget, lengthscale):
    vmem = pl.BlockSpec(memory_space=pltpu.VMEM)
    f32 = jnp.float32
    return pl.pallas_call(
        factor_kernel,
        out_shape=(
            jax.ShapeDtypeStruct((RB, PB), f32),
            jax.ShapeDtypeStruct((RB, PB), f32),
        ),
        in_specs=[pl.BlockSpec(memory_space=pltpu.SMEM)] + [vmem] * 6,
        out_specs=(vmem, vmem),
        scratch_shapes=[
            pltpu.VMEM((RB, F), f32),
            pltpu.VMEM((PB, F), f32),
            pltpu.VMEM((PB, F), f32),
            pltpu.VMEM((8, PB), f32),
            pltpu.VMEM((PB, PB + RB), f32),
            pltpu.VMEM((PB, PB), f32),
            pltpu.VMEM((PB, RB), f32),
            pltpu.VMEM((RB, RB), f32),
        ],
        compiler_params=pltpu.CompilerParams(vmem_limit_bytes=48 * 1024 * 1024),
        name="factor",
    )(where, blk, col, pan, pnug, nugget.reshape(1, RB), lengthscale.reshape(1, F))


def body(telemetry, target, counts, lengthscale, nugget):
    block_pts, col_packed, pan_packed, pnug = exchange(telemetry, target, counts, nugget)
    where = jnp.stack([lax.axis_index("row"), lax.axis_index("col")]).astype(jnp.int32)
    schur_tile, row_lower = factor_and_update(
        where, block_pts, col_packed, pan_packed, pnug, nugget, lengthscale
    )
    return (schur_tile[:, None, :], row_lower)


def solution(mesh):
    in_specs = (P("col", "row", None), P("col", "row"), P("col", "row"), P(), P("row"))
    out_specs = (P("row", "col", None), P("row", None))
    return jax.shard_map(body, mesh=mesh, in_specs=in_specs, out_specs=out_specs, check_vma=False)
```

```python
import functools

import jax
import jax.numpy as jnp
from jax import lax
from jax.experimental import pallas as pl
from jax.experimental.pallas import tpu as pltpu
from jax.sharding import PartitionSpec as P

F = 64
PB = 1024
RB = 128
NR = 64
NC = 8
SL = 16
WIN = 16
SLOTS = 32
HI = lax.Precision.HIGHEST
MESH = pl.DeviceIdType.MESH

root_three = 1.7320508075688772


def hdot(a, b):
    return jnp.dot(a, b, precision=HI, preferred_element_type=jnp.float32)


def exchange_kernel(
    tel_ref, tgt_ref, cnt_ref, nug_ref,
    blk_ref, col_ref, pan_ref, pnug_ref,
    out1, in1, comp, gath, mine, nugtile,
    s1, r1, s2, r2, s3, r3, s4, r4, s5, r5,
):
    r = lax.axis_index("row")
    c = lax.axis_index("col")

    def at_row(peer):
        return (peer, c)

    def at_col(peer):
        return (r, peer)

    barrier = pltpu.get_barrier_semaphore()

    def greet_row(i, carry):
        pl.semaphore_signal(
            barrier, inc=1, device_id=at_row(lax.rem(r + i, NR)), device_id_type=MESH
        )
        return carry

    def greet_col(i, carry):
        pl.semaphore_signal(
            barrier, inc=1, device_id=at_col(lax.rem(c + i, NC)), device_id_type=MESH
        )
        return carry

    lax.fori_loop(1, NR, greet_row, 0)
    lax.fori_loop(1, NC, greet_col, 0)

    tel = tel_ref[0]
    t_row = tgt_ref[...]
    sub = lax.broadcasted_iota(jnp.int32, (SLOTS, SLOTS), 0)
    lane = lax.broadcasted_iota(jnp.int32, (SLOTS, SLOTS), 1)
    t_mat = jnp.broadcast_to(t_row, (SLOTS, SLOTS))
    t_col = jnp.sum(jnp.where(sub == lane, t_mat, 0), axis=1, keepdims=True)
    zone_row = lax.shift_right_logical(t_row, 7)
    zone_col = lax.shift_right_logical(t_col, 7)
    filled = cnt_ref[...]
    earlier = (zone_col == zone_row) & (sub < filled) & (sub < lane)
    position = jnp.sum(earlier.astype(jnp.int32), axis=0, keepdims=True)
    offset = jnp.bitwise_and(r - zone_row + NR, NR - 1)
    used = (lane[0:1] < filled) & (position < 2) & (offset < WIN)
    slot = jnp.where(used, offset * 2 + position, -1)
    place = jnp.bitwise_and(t_row, RB - 1).astype(jnp.float32)
    dist = lax.broadcasted_iota(jnp.int32, (WIN, SLOTS), 0) * 2
    pick0 = dist == slot
    pick1 = dist + 1 == slot
    feat0 = hdot(pick0.astype(jnp.float32), tel)
    feat1 = hdot(pick1.astype(jnp.float32), tel)
    place0 = jnp.max(jnp.where(pick0, place, -1.0), axis=1, keepdims=True)
    place1 = jnp.max(jnp.where(pick1, place, -1.0), axis=1, keepdims=True)
    feats = jnp.concatenate([feat0, feat1], axis=1)
    lane_w = lax.broadcasted_iota(jnp.int32, (WIN, 128), 1)
    places = jnp.where(lane_w < F, place0, place1)
    tile_row = lax.broadcasted_iota(jnp.int32, (8, 128), 0)
    for d in range(WIN):
        out1[d] = jnp.where(
            tile_row == 0, feats[d : d + 1], jnp.where(tile_row == 1, places[d : d + 1], 0.0)
        )
    in1[0] = out1[0]
    nugtile[...] = jnp.broadcast_to(nug_ref[...], (8, 128))

    pl.semaphore_wait(barrier, NR - 1 + NC - 1)

    def step1(d):
        return pltpu.make_async_remote_copy(
            src_ref=out1.at[d], dst_ref=in1.at[d], send_sem=s1.at[d], recv_sem=r1.at[d],
            device_id=at_row(lax.rem(r - d + NR, NR)), device_id_type=MESH,
        )

    def start1(d, carry):
        step1(d).start()
        return carry

    lax.fori_loop(1, WIN, start1, 0)

    def step5(i, slot_id):
        return pltpu.make_async_remote_copy(
            src_ref=nugtile, dst_ref=pnug_ref.at[slot_id], send_sem=s5.at[i],
            recv_sem=r5.at[slot_id],
            device_id=at_row(lax.rem(r + i, NR)), device_id_type=MESH,
        )

    @pl.when(r < NC)
    def _():
        def start5(i, carry):
            step5(i, r).start()
            return carry

        lax.fori_loop(1, NR, start5, 0)
        pnug_ref[r] = nugtile[...]

    def wait1(d, carry):
        step1(d).wait_recv()
        return carry

    lax.fori_loop(1, WIN, wait1, 0)
    o = lax.broadcasted_iota(jnp.int32, (2 * WIN, 128), 0)
    k = lax.broadcasted_iota(jnp.int32, (2 * WIN, 128), 1)
    chosen = k == jnp.where(o < WIN, 8 * o, 8 * (o - WIN) + 1)
    comp[...] = hdot(chosen.astype(jnp.float32), in1[...].reshape(WIN * 8, 128))
    gath[c] = comp[...]

    def step2(i, slot_id):
        return pltpu.make_async_remote_copy(
            src_ref=comp, dst_ref=gath.at[slot_id], send_sem=s2.at[i], recv_sem=r2.at[slot_id],
            device_id=at_col(lax.rem(c + i, NC)), device_id_type=MESH,
        )

    for i in range(1, NC):
        step2(i, c).start()
    for i in range(1, NC):
        step2(i, lax.rem(c + i, NC)).wait_recv()

    all_feats = gath[:, 0:WIN, :].reshape(NC * WIN, 128)
    all_places = gath[:, WIN : 2 * WIN, :].reshape(NC * WIN, 128)
    spot = lax.broadcasted_iota(jnp.int32, (NC * WIN, RB), 1).astype(jnp.float32)
    put0 = (all_places[:, 0:1] == spot).astype(jnp.float32)
    put1 = (all_places[:, F : F + 1] == spot).astype(jnp.float32)
    blk_ref[...] = hdot(put0.T, all_feats[:, 0:F]) + hdot(put1.T, all_feats[:, F : 2 * F])

    mine[:, 0:F] = blk_ref[pl.ds(c * SL, 8), :]
    mine[:, F : 2 * F] = blk_ref[pl.ds(c * SL + 8, 8), :]
    col_ref[r] = mine[...]

    def step3(i, slot_id):
        return pltpu.make_async_remote_copy(
            src_ref=mine, dst_ref=col_ref.at[slot_id], send_sem=s3.at[i], recv_sem=r3.at[slot_id],
            device_id=at_row(lax.rem(r + i, NR)), device_id_type=MESH,
        )

    def start3(i, carry):
        step3(i, r).start()
        return carry

    lax.fori_loop(1, NR, start3, 0)

    def wait3(slot_id):
        @pl.when(slot_id != r)
        def _():
            step3(1, slot_id).wait_recv()

    for slot_id in range(NC):
        wait3(slot_id)

    def step4(i, slot_id):
        return pltpu.make_async_remote_copy(
            src_ref=col_ref.at[pl.ds(0, NC)], dst_ref=pan_ref.at[slot_id], send_sem=s4.at[i],
            recv_sem=r4.at[slot_id],
            device_id=at_col(lax.rem(c + i, NC)), device_id_type=MESH,
        )

    for i in range(1, NC):
        step4(i, c).start()
    pan_ref[c] = col_ref[0:NC]

    def rest3(slot_id, carry):
        wait3(slot_id)
        return carry

    lax.fori_loop(NC, NR, rest3, 0)
    for slot_id in range(NC):
        @pl.when(slot_id != r)
        def _(slot_id=slot_id):
            step5(1, slot_id).wait_recv()

    for i in range(1, NC):
        step4(i, lax.rem(c + i, NC)).wait_recv()

    def sent1(d, carry):
        step1(d).wait_send()
        return carry

    lax.fori_loop(1, WIN, sent1, 0)
    for i in range(1, NC):
        step2(i, c).wait_send()
        step4(i, c).wait_send()

    def sent3(i, carry):
        step3(i, r).wait_send()
        return carry

    lax.fori_loop(1, NR, sent3, 0)

    @pl.when(r < NC)
    def _():
        def sent5(i, carry):
            step5(i, r).wait_send()
            return carry

        lax.fori_loop(1, NR, sent5, 0)


def exchange(telemetry, target, counts, nugget):
    dma = pltpu.SemaphoreType.DMA
    vmem = pl.BlockSpec(memory_space=pltpu.VMEM)
    f32 = jnp.float32
    return pl.pallas_call(
        exchange_kernel,
        out_shape=(
            jax.ShapeDtypeStruct((RB, F), f32),
            jax.ShapeDtypeStruct((NR, 8, 128), f32),
            jax.ShapeDtypeStruct((NC, NC, 8, 128), f32),
            jax.ShapeDtypeStruct((NC, 8, 128), f32),
        ),
        in_specs=[vmem] * 4,
        out_specs=(vmem,) * 4,
        scratch_shapes=[
            pltpu.VMEM((WIN, 8, 128), f32),
            pltpu.VMEM((WIN, 8, 128), f32),
            pltpu.VMEM((2 * WIN, 128), f32),
            pltpu.VMEM((NC, 2 * WIN, 128), f32),
            pltpu.VMEM((8, 128), f32),
            pltpu.VMEM((8, 128), f32),
            dma((WIN,)), dma((WIN,)), dma((NC,)), dma((NC,)), dma((NR,)), dma((NR,)),
            dma((NC,)), dma((NC,)), dma((NR,)), dma((NC,)),
        ],
        compiler_params=pltpu.CompilerParams(
            collective_id=0, has_side_effects=True, vmem_limit_bytes=32 * 1024 * 1024
        ),
        name="exchange",
    )(telemetry, target, counts, nugget.reshape(1, RB))


def sublanes(x, i):
    return jnp.broadcast_to(x[i : i + 1, :], (8, RB))


def lanes(x, j):
    return lax.gather(
        x,
        jnp.full((8, RB, 1), j, jnp.int32),
        lax.GatherDimensionNumbers(
            offset_dims=(), collapsed_slice_dims=(1,), start_index_map=(1,),
            operand_batching_dims=(0,), start_indices_batching_dims=(0,),
        ),
        slice_sizes=(1, 1),
        mode=lax.GatherScatterMode.PROMISE_IN_BOUNDS,
    )


def parts(x):
    f32 = jnp.float32
    hi = x.astype(jnp.bfloat16)
    rest = x - hi.astype(f32)
    mid = rest.astype(jnp.bfloat16)
    low = (rest - mid.astype(f32)).astype(jnp.bfloat16)
    return hi, mid, low


def left_stack(p, axis=0):
    hi, mid, low = p
    return jnp.concatenate([hi, hi, hi, mid, mid, low], axis=axis)


def right_stack(p):
    hi, mid, low = p
    return jnp.concatenate([hi, mid, low, hi, mid, hi], axis=0)


def stacked(left, right, over=0):
    return lax.dot_general(
        left, right, (((over,), (0,)), ((), ())), preferred_element_type=jnp.float32
    )


def gram(u):
    f32 = jnp.float32
    hi = u.astype(jnp.bfloat16).astype(f32)
    rest = u - hi
    mid = rest.astype(jnp.bfloat16).astype(f32)
    low = rest - mid
    left = jnp.concatenate([hi, hi, hi, mid, mid, low], axis=0).astype(jnp.bfloat16)
    right = jnp.concatenate([hi, mid, low, hi, mid, hi], axis=0).astype(jnp.bfloat16)
    return stacked(left, right)


AHEAD = 3


def factor_block(groups, fill):
    groups = list(groups)
    count = len(groups)
    sub = lax.broadcasted_iota(jnp.int32, (8, RB), 0)
    lane = lax.broadcasted_iota(jnp.int32, (8, RB), 1)
    for g in range(count):
        first = 8 * g
        near = list(range(g, min(count, g + AHEAD)))
        cols = {h: [lanes(groups[h], first + k) for k in range(8)] for h in near}
        in_panel = (lane >= first) & (lane < first + 8)
        one = (lane - first == sub).astype(jnp.float32)
        for h in range(g, count):
            groups[h] = jnp.where(in_panel, one if h == g else 0.0, groups[h])
        pivots = jnp.ones((8, RB), jnp.float32)
        small = [[sublanes(cols[g][k], i) if k >= i else None for k in range(8)] for i in range(8)]
        for i in range(8):
            fill(8 * g + i)
            inv = pl.reciprocal(small[i][i], approx=True)
            inv = inv * (2.0 - small[i][i] * inv)
            pivots = jnp.where(sub == i, small[i][i], pivots)
            row = sublanes(groups[g], i)
            for j in range(i + 1, 8):
                scale = small[i][j] * inv
                for k in range(j, 8):
                    small[j][k] = small[j][k] - scale * small[i][k]
            for h in near:
                step = cols[h][i] * inv
                if h == g:
                    step = jnp.where(sub > i, step, 0.0)
                for k in range(i + 1, 8):
                    cols[h][k] = cols[h][k] - step * small[i][k]
                if h != g or i < 7:
                    groups[h] = groups[h] - step * row
        done = groups[g] * lax.rsqrt(pivots)
        groups[g] = done
        if g + AHEAD < count:
            product = gram(done)
            for h in range(g + AHEAD, count):
                groups[h] = groups[h] - product[8 * h : 8 * h + 8, :]
    return groups


def tdot(a, b):
    return lax.dot_general(
        a, b, (((0,), (0,)), ((), ())), precision=HI, preferred_element_type=jnp.float32
    )


def matern(left, left_sq, right, right_sq):
    squared = left_sq + right_sq - 2.0 * stacked(left, right)
    scaled = root_three * jnp.sqrt(jnp.maximum(squared, 0.0))
    return (1.0 + scaled) * jnp.exp(-scaled)


def spread(jobs, slots):
    def fill(slot):
        for job in jobs[slot * len(jobs) // slots : (slot + 1) * len(jobs) // slots]:
            job()

    return fill


WIDTH = PB + RB


def factor_kernel(
    where_ref, blk_ref, col_ref, pan_ref, pnug_ref, nug_ref, len_ref,
    schur_ref, lower_ref,
    pts, cpts, nugs, sq_l, sq_r, sq_c, p_l, p_r, c_r, big, across, weights, u_ref,
):
    r = where_ref[0]
    c = where_ref[1]
    inv = 1.0 / len_ref[...]
    pts[PB:, :] = blk_ref[...] * inv
    for rb in range(NC):
        nugs[:, rb * RB : (rb + 1) * RB] = pnug_ref[rb]
        for cc in range(NC):
            at = rb * RB + cc * SL
            both = pan_ref[cc, rb]
            pts[at : at + 8, :] = both[:, 0:F] * inv
            pts[at + 8 : at + SL, :] = both[:, F : 2 * F] * inv
    for rb in range(NR):
        both = col_ref[rb]
        cpts[rb * SL : rb * SL + 8, :] = both[:, 0:F] * inv
        cpts[rb * SL + 8 : rb * SL + SL, :] = both[:, F : 2 * F] * inv
    for i in range(NC + 1):
        at = i * RB
        block = pts[at : at + RB, :]
        turned = block.T
        sq_l[at : at + RB, :] = jnp.sum(block * block, axis=1, keepdims=True)
        sq_r[:, at : at + RB] = jnp.sum(turned * turned, axis=0, keepdims=True)
        p = parts(turned)
        p_l[:, at : at + RB] = left_stack(p)
        p_r[:, at : at + RB] = right_stack(p)
    for i in range(NC):
        at = i * RB
        turned = cpts[at : at + RB, :].T
        sq_c[:, at : at + RB] = jnp.sum(turned * turned, axis=0, keepdims=True)
        c_r[:, at : at + RB] = right_stack(parts(turned))

    eye = lax.broadcasted_iota(jnp.int32, (RB, RB), 0) == lax.broadcasted_iota(
        jnp.int32, (RB, RB), 1
    )
    low = lax.broadcasted_iota(jnp.int32, (RB, RB), 0) >= lax.broadcasted_iota(
        jnp.int32, (RB, RB), 1
    )
    sub = lax.broadcasted_iota(jnp.int32, (RB, 1), 0)

    def column_ids(start, width):
        n = start + lax.broadcasted_iota(jnp.int32, (1, width), 1)
        return lax.shift_right_logical(n, 4) * RB + c * SL + jnp.bitwise_and(n, SL - 1)

    def panel_job(i, lo, hi):
        def job():
            at = i * RB
            block = matern(
                p_l[:, at : at + RB], sq_l[at : at + RB, :], p_r[:, lo:hi], sq_r[:, lo:hi]
            )
            if lo == at:
                block = block + jnp.where(eye, nugs[0:1, at : at + RB], 0.0)
            if lo == PB:
                same = jnp.where(r == i, 1.0, 0.0)
                block = block + same * jnp.where(eye, nugs[0:1, at : at + RB], 0.0)
            big[at : at + RB, lo:hi] = block

        return job

    def across_job(i, lo, hi):
        def job():
            at = i * RB
            block = matern(
                p_l[:, at : at + RB], sq_l[at : at + RB, :], c_r[:, lo:hi], sq_c[:, lo:hi]
            )
            if lo < RB:
                nug_col = jnp.sum(
                    jnp.where(eye, nugs[0:1, at : at + RB], 0.0), axis=1, keepdims=True
                )
                block = block + jnp.where(at + sub == column_ids(lo, hi - lo), nug_col, 0.0)
            across[at : at + RB, lo:hi] = block

        return job

    def keep(half, lo, hi, value):
        hi_p, mid_p, low_p = parts(value)
        u_ref[half, 0, :, lo:hi] = hi_p
        u_ref[half, 1, :, lo:hi] = mid_p
        u_ref[half, 2, :, lo:hi] = low_p

    def kept(half, lo, hi):
        return tuple(u_ref[half, q, :, lo:hi] for q in range(3))

    def row_job(k, left, lo, hi):
        def job():
            at = k * RB
            value = stacked(left, right_stack(parts(big[at : at + RB, lo:hi])), 1)
            big[at : at + RB, lo:hi] = value
            keep(k % 2, lo, hi, value)

        return job

    def update_job(k, i, lo, hi):
        def job():
            at = i * RB
            change = stacked(
                left_stack(kept(k % 2, at, at + RB)), right_stack(kept(k % 2, lo, hi))
            )
            if lo == k * RB:
                big[at : at + RB, lo:hi] = -change
            else:
                big[at : at + RB, lo:hi] = big[at : at + RB, lo:hi] - change

        return job

    def pieces(lo, hi, size=2 * RB):
        return [(x, min(hi, x + size)) for x in range(lo, hi, size)]

    panel_job(0, 0, RB)()
    jobs = []
    for i in range(NC):
        spans = pieces((i if i else 1) * RB, PB) if i == 0 else [(i * RB, (i + 1) * RB)]
        if i:
            spans = spans + pieces((i + 1) * RB, PB)
        jobs += [panel_job(i, lo, hi) for lo, hi in spans + [(PB, WIDTH)]]
    extra = {3: (0, 6), 4: (6, 13), 5: (13, 20), 6: (20, 26), 7: (26, 32)}
    slices = [(i, lo, hi) for i in range(NC) for lo, hi in pieces(0, PB)]
    square = big[0:RB, 0:RB]
    for k in range(NC):
        at = k * RB
        if k in extra:
            jobs += [across_job(*x) for x in slices[extra[k][0] : extra[k][1]]]
        groups = factor_block([square[h : h + 8, :] for h in range(0, RB, 8)], spread(jobs, RB))
        inverse = jnp.where(low, jnp.concatenate(groups, axis=0), 0.0)
        left = left_stack(parts(inverse), axis=1)
        nxt = at + RB
        if k < NC - 1:
            beside = stacked(left, right_stack(parts(big[at:nxt, nxt : nxt + RB])), 1)
            p = parts(beside)
            square = big[nxt : nxt + RB, nxt : nxt + RB] - stacked(left_stack(p), right_stack(p))
            keep(k % 2, nxt, nxt + RB, beside)
        big[at:nxt, at:nxt] = inverse
        keep(k % 2, at, nxt, inverse)
        jobs = [row_job(k, left, lo, hi) for lo, hi in pieces(0, at)]
        jobs += [row_job(k, left, lo, hi) for lo, hi in pieces(min(nxt + RB, PB), WIDTH)]
        for i in range(k + 1, NC):
            start = (i if i > k + 1 else i + 1) * RB
            spans = pieces(0, at) + [(at, nxt)] + pieces(start, WIDTH)
            jobs += [update_job(k, i, lo, hi) for lo, hi in spans]
    for job in jobs:
        job()

    for j in range(NC):
        at = j * RB
        weights[at : at + RB, :] = tdot(big[at:, at : at + RB], big[at:, PB:])
        lower_ref[:, at : at + RB] = big[at : at + RB, PB:].T
    nug_own = jnp.sum(jnp.where(eye, nug_ref[...], 0.0), axis=1, keepdims=True)
    schur_ref[...] = (
        matern(p_l[:, PB:], sq_l[PB:, :], c_r[...], sq_c[...])
        + jnp.where(r * RB + sub == column_ids(0, PB), nug_own, 0.0)
        - tdot(weights[...], across[...])
    )


def factor_and_update(where, blk, col, pan, pnug, nugget, lengthscale):
    vmem = pl.BlockSpec(memory_space=pltpu.VMEM)
    f32 = jnp.float32
    return pl.pallas_call(
        factor_kernel,
        out_shape=(
            jax.ShapeDtypeStruct((RB, PB), f32),
            jax.ShapeDtypeStruct((RB, PB), f32),
        ),
        in_specs=[pl.BlockSpec(memory_space=pltpu.SMEM)] + [vmem] * 6,
        out_specs=(vmem, vmem),
        scratch_shapes=[
            pltpu.VMEM((WIDTH, F), f32),
            pltpu.VMEM((PB, F), f32),
            pltpu.VMEM((8, PB), f32),
            pltpu.VMEM((WIDTH, 1), f32),
            pltpu.VMEM((1, WIDTH), f32),
            pltpu.VMEM((1, PB), f32),
            pltpu.VMEM((6 * F, WIDTH), jnp.bfloat16),
            pltpu.VMEM((6 * F, WIDTH), jnp.bfloat16),
            pltpu.VMEM((6 * F, PB), jnp.bfloat16),
            pltpu.VMEM((PB, WIDTH), f32),
            pltpu.VMEM((PB, PB), f32),
            pltpu.VMEM((PB, RB), f32),
            pltpu.VMEM((2, 3, RB, WIDTH), jnp.bfloat16),
        ],
        compiler_params=pltpu.CompilerParams(vmem_limit_bytes=48 * 1024 * 1024),
        name="factor",
    )(where, blk, col, pan, pnug, nugget.reshape(1, RB), lengthscale.reshape(1, F))


def body(telemetry, target, counts, lengthscale, nugget):
    block_pts, col_packed, pan_packed, pnug = exchange(telemetry, target, counts, nugget)
    where = jnp.stack([lax.axis_index("row"), lax.axis_index("col")]).astype(jnp.int32)
    schur_tile, row_lower = factor_and_update(
        where, block_pts, col_packed, pan_packed, pnug, nugget, lengthscale
    )
    return (schur_tile[:, None, :], row_lower)


def solution(mesh):
    in_specs = (P("col", "row", None), P("col", "row"), P("col", "row"), P(), P("row"))
    out_specs = (P("row", "col", None), P("row", None))
    return jax.shard_map(body, mesh=mesh, in_specs=in_specs, out_specs=out_specs, check_vma=False)
```

```python
import functools

import jax
import jax.numpy as jnp
from jax import lax
from jax.experimental import pallas as pl
from jax.experimental.pallas import tpu as pltpu
from jax.sharding import PartitionSpec as P

F = 64
PB = 1024
RB = 128
NR = 64
NC = 8
SL = 16
WIN = 16
SLOTS = 32
HI = lax.Precision.HIGHEST
MESH = pl.DeviceIdType.MESH

root_three = 1.7320508075688772


def hdot(a, b):
    return jnp.dot(a, b, precision=HI, preferred_element_type=jnp.float32)


def exchange_kernel(
    tel_ref, tgt_ref, cnt_ref, nug_ref,
    blk_ref, col_ref, pan_ref, pnug_ref,
    out1, in1, comp, gath, mine, nugtile,
    s1, r1, s2, r2, s3, r3, s4, r4, s5, r5,
):
    r = lax.axis_index("row")
    c = lax.axis_index("col")

    def at_row(peer):
        return (peer, c)

    def at_col(peer):
        return (r, peer)

    barrier = pltpu.get_barrier_semaphore()

    def greet_row(i, carry):
        pl.semaphore_signal(
            barrier, inc=1, device_id=at_row(lax.rem(r + i, NR)), device_id_type=MESH
        )
        return carry

    def greet_col(i, carry):
        pl.semaphore_signal(
            barrier, inc=1, device_id=at_col(lax.rem(c + i, NC)), device_id_type=MESH
        )
        return carry

    lax.fori_loop(1, NR, greet_row, 0)
    lax.fori_loop(1, NC, greet_col, 0)

    tel = tel_ref[0]
    t_row = tgt_ref[...]
    sub = lax.broadcasted_iota(jnp.int32, (SLOTS, SLOTS), 0)
    lane = lax.broadcasted_iota(jnp.int32, (SLOTS, SLOTS), 1)
    t_mat = jnp.broadcast_to(t_row, (SLOTS, SLOTS))
    t_col = jnp.sum(jnp.where(sub == lane, t_mat, 0), axis=1, keepdims=True)
    zone_row = lax.shift_right_logical(t_row, 7)
    zone_col = lax.shift_right_logical(t_col, 7)
    filled = cnt_ref[...]
    earlier = (zone_col == zone_row) & (sub < filled) & (sub < lane)
    position = jnp.sum(earlier.astype(jnp.int32), axis=0, keepdims=True)
    offset = jnp.bitwise_and(r - zone_row + NR, NR - 1)
    used = (lane[0:1] < filled) & (position < 2) & (offset < WIN)
    slot = jnp.where(used, offset * 2 + position, -1)
    place = jnp.bitwise_and(t_row, RB - 1).astype(jnp.float32)
    dist = lax.broadcasted_iota(jnp.int32, (WIN, SLOTS), 0) * 2
    pick0 = dist == slot
    pick1 = dist + 1 == slot
    feat0 = hdot(pick0.astype(jnp.float32), tel)
    feat1 = hdot(pick1.astype(jnp.float32), tel)
    place0 = jnp.max(jnp.where(pick0, place, -1.0), axis=1, keepdims=True)
    place1 = jnp.max(jnp.where(pick1, place, -1.0), axis=1, keepdims=True)
    feats = jnp.concatenate([feat0, feat1], axis=1)
    lane_w = lax.broadcasted_iota(jnp.int32, (WIN, 128), 1)
    places = jnp.where(lane_w < F, place0, place1)
    tile_row = lax.broadcasted_iota(jnp.int32, (8, 128), 0)
    for d in range(WIN):
        out1[d] = jnp.where(
            tile_row == d % 8,
            feats[d : d + 1],
            jnp.where(tile_row == (d + 4) % 8, places[d : d + 1], 0.0),
        )
    in1[0] = out1[0]
    nugtile[...] = jnp.broadcast_to(nug_ref[...], (8, 128))

    pl.semaphore_wait(barrier, NR - 1 + NC - 1)

    def step1(d):
        return pltpu.make_async_remote_copy(
            src_ref=out1.at[d], dst_ref=in1.at[d], send_sem=s1, recv_sem=r1,
            device_id=at_row(jnp.bitwise_and(r - d + NR, NR - 1)), device_id_type=MESH,
        )

    def start1(d, carry):
        step1(d).start()
        return carry

    lax.fori_loop(1, WIN, start1, 0)

    def drain(ref, sem):
        pltpu.make_async_copy(ref, ref, sem).wait()

    def step5(i, slot_id):
        return pltpu.make_async_remote_copy(
            src_ref=nugtile, dst_ref=pnug_ref.at[slot_id], send_sem=s5, recv_sem=r5,
            device_id=at_row(jnp.bitwise_and(r + i, NR - 1)), device_id_type=MESH,
        )

    drain(in1.at[pl.ds(1, WIN - 1)], r1)
    for half in range(2):
        feat_rows = jnp.zeros((8, 128), jnp.float32)
        place_rows = jnp.zeros((8, 128), jnp.float32)
        for d in range(8):
            got = in1[8 * half + d]
            feat_rows = jnp.where(tile_row == d, got, feat_rows)
            place_rows = jnp.where(tile_row == (d + 4) % 8, got, place_rows)
        comp[8 * half : 8 * half + 8, :] = feat_rows
        comp[WIN + 8 * half : WIN + 8 * half + 8, :] = pltpu.roll(place_rows, 4, 0)

    def step2(i, slot_id):
        return pltpu.make_async_remote_copy(
            src_ref=comp, dst_ref=gath.at[slot_id], send_sem=s2, recv_sem=r2,
            device_id=at_col(jnp.bitwise_and(c + i, NC - 1)), device_id_type=MESH,
        )

    for i in range(1, NC):
        step2(i, c).start()
    gath[c] = comp[...]

    @pl.when(r < NC)
    def _():
        def start5(i, carry):
            step5(i, r).start()
            return carry

        lax.fori_loop(1, NR, start5, 0)
        pnug_ref[r] = nugtile[...]

    drain(gath.at[pl.ds(1, NC - 1)], r2)

    all_feats = gath[:, 0:WIN, :].reshape(NC * WIN, 128)
    all_places = gath[:, WIN : 2 * WIN, :].reshape(NC * WIN, 128)
    hi_p, mid_p, low_p = parts(all_feats)
    stack = jnp.concatenate([hi_p, mid_p, low_p], axis=0)

    def placed(first, count):
        spot = first + lax.broadcasted_iota(jnp.int32, (NC * WIN, count), 1)
        spot = spot.astype(jnp.float32)
        put0 = (all_places[:, 0:1] == spot).astype(jnp.bfloat16)
        put1 = (all_places[:, F : F + 1] == spot).astype(jnp.bfloat16)
        rows0 = stacked(jnp.concatenate([put0] * 3, axis=0), stack)
        rows1 = stacked(jnp.concatenate([put1] * 3, axis=0), stack)
        return rows0[:, 0:F] + rows1[:, F : 2 * F]

    group = placed(c * SL, SL)
    mine[:, 0:F] = group[0:8]
    mine[:, F : 2 * F] = group[8:SL]

    late = (r >= NC).astype(jnp.int32)

    def step3(i, slot_id):
        return pltpu.make_async_remote_copy(
            src_ref=mine, dst_ref=col_ref.at[slot_id], send_sem=s3, recv_sem=r3.at[late],
            device_id=at_row(jnp.bitwise_and(r + i, NR - 1)), device_id_type=MESH,
        )

    def start3(i, carry):
        step3(i, r).start()
        return carry

    lax.fori_loop(1, NR, start3, 0)
    col_ref[r] = mine[...]
    blk_ref[...] = placed(0, RB)

    @pl.when(r < NC)
    def _():
        drain(col_ref.at[pl.ds(0, NC - 1)], r3.at[0])

    @pl.when(r >= NC)
    def _():
        drain(col_ref.at[pl.ds(0, NC)], r3.at[0])

    def step4(i, slot_id):
        return pltpu.make_async_remote_copy(
            src_ref=col_ref.at[pl.ds(0, NC)], dst_ref=pan_ref.at[slot_id], send_sem=s4,
            recv_sem=r4,
            device_id=at_col(jnp.bitwise_and(c + i, NC - 1)), device_id_type=MESH,
        )

    for i in range(1, NC):
        step4(i, c).start()
    pan_ref[c] = col_ref[0:NC]

    @pl.when(r < NC)
    def _():
        drain(col_ref.at[pl.ds(NC, NR - NC)], r3.at[1])
        drain(pnug_ref.at[pl.ds(0, NC - 1)], r5)

    @pl.when(r >= NC)
    def _():
        drain(col_ref.at[pl.ds(NC, NR - NC - 1)], r3.at[1])
        drain(pnug_ref, r5)

    drain(in1.at[pl.ds(1, WIN - 1)], s1)
    drain(gath.at[pl.ds(1, NC - 1)], s2)
    drain(col_ref.at[pl.ds(1, NR - 1)], s3)
    drain(pan_ref.at[pl.ds(1, NC - 1)], r4)
    drain(pan_ref.at[pl.ds(1, NC - 1)], s4)

    @pl.when(r < NC)
    def _():
        drain(col_ref.at[pl.ds(1, NR - 1)], s5)


def exchange(telemetry, target, counts, nugget):
    dma = pltpu.SemaphoreType.DMA
    vmem = pl.BlockSpec(memory_space=pltpu.VMEM)
    f32 = jnp.float32
    return pl.pallas_call(
        exchange_kernel,
        out_shape=(
            jax.ShapeDtypeStruct((RB, F), f32),
            jax.ShapeDtypeStruct((NR, 8, 128), f32),
            jax.ShapeDtypeStruct((NC, NC, 8, 128), f32),
            jax.ShapeDtypeStruct((NC, 8, 128), f32),
        ),
        in_specs=[vmem] * 4,
        out_specs=(vmem,) * 4,
        scratch_shapes=[
            pltpu.VMEM((WIN, 8, 128), f32),
            pltpu.VMEM((WIN, 8, 128), f32),
            pltpu.VMEM((2 * WIN, 128), f32),
            pltpu.VMEM((NC, 2 * WIN, 128), f32),
            pltpu.VMEM((8, 128), f32),
            pltpu.VMEM((8, 128), f32),
            dma(()), dma(()), dma(()), dma(()), dma(()), dma((2,)),
            dma(()), dma(()), dma(()), dma(()),
        ],
        compiler_params=pltpu.CompilerParams(
            collective_id=0, has_side_effects=True, vmem_limit_bytes=32 * 1024 * 1024
        ),
        name="exchange",
    )(telemetry, target, counts, nugget.reshape(1, RB))


def sublanes(x, i):
    return jnp.broadcast_to(x[i : i + 1, :], (8, RB))


def lanes(x, j):
    return lax.gather(
        x,
        jnp.full((8, RB, 1), j, jnp.int32),
        lax.GatherDimensionNumbers(
            offset_dims=(), collapsed_slice_dims=(1,), start_index_map=(1,),
            operand_batching_dims=(0,), start_indices_batching_dims=(0,),
        ),
        slice_sizes=(1, 1),
        mode=lax.GatherScatterMode.PROMISE_IN_BOUNDS,
    )


def parts(x):
    f32 = jnp.float32
    hi = x.astype(jnp.bfloat16)
    rest = x - hi.astype(f32)
    mid = rest.astype(jnp.bfloat16)
    low = (rest - mid.astype(f32)).astype(jnp.bfloat16)
    return hi, mid, low


def left_stack(p, axis=0):
    hi, mid, low = p
    return jnp.concatenate([hi, hi, hi, mid, mid, low], axis=axis)


def right_stack(p):
    hi, mid, low = p
    return jnp.concatenate([hi, mid, low, hi, mid, hi], axis=0)


def left_short(p):
    return jnp.concatenate([p[0], p[0], p[1]], axis=0)


def right_short(p):
    return jnp.concatenate([p[0], p[1], p[0]], axis=0)


def stacked(left, right, over=0):
    return lax.dot_general(
        left, right, (((over,), (0,)), ((), ())), preferred_element_type=jnp.float32
    )


def gram(u):
    f32 = jnp.float32
    hi = u.astype(jnp.bfloat16).astype(f32)
    rest = u - hi
    mid = rest.astype(jnp.bfloat16).astype(f32)
    low = rest - mid
    left = jnp.concatenate([hi, hi, hi, mid, mid, low], axis=0).astype(jnp.bfloat16)
    right = jnp.concatenate([hi, mid, low, hi, mid, hi], axis=0).astype(jnp.bfloat16)
    return stacked(left, right)


AHEAD = 3


def factor_block(groups, fill):
    groups = list(groups)
    count = len(groups)
    sub = lax.broadcasted_iota(jnp.int32, (8, RB), 0)
    lane = lax.broadcasted_iota(jnp.int32, (8, RB), 1)
    for g in range(count):
        first = 8 * g
        near = list(range(g, min(count, g + AHEAD)))
        cols = {h: [lanes(groups[h], first + k) for k in range(8)] for h in near}
        in_panel = (lane >= first) & (lane < first + 8)
        one = (lane - first == sub).astype(jnp.float32)
        for h in range(g, count):
            groups[h] = jnp.where(in_panel, one if h == g else 0.0, groups[h])
        pivots = jnp.ones((8, RB), jnp.float32)
        small = [[sublanes(cols[g][k], i) if k >= i else None for k in range(8)] for i in range(8)]
        for i in range(8):
            fill(8 * g + i)
            inv = pl.reciprocal(small[i][i], approx=True)
            inv = inv * (2.0 - small[i][i] * inv)
            pivots = jnp.where(sub == i, small[i][i], pivots)
            row = sublanes(groups[g], i)
            for j in range(i + 1, 8):
                scale = small[i][j] * inv
                for k in range(j, 8):
                    small[j][k] = small[j][k] - scale * small[i][k]
            for h in near:
                step = cols[h][i] * inv
                if h == g:
                    step = jnp.where(sub > i, step, 0.0)
                for k in range(i + 1, 8):
                    cols[h][k] = cols[h][k] - step * small[i][k]
                if h != g or i < 7:
                    groups[h] = groups[h] - step * row
        done = groups[g] * lax.rsqrt(pivots)
        groups[g] = done
        if g + AHEAD < count:
            product = gram(done)
            for h in range(g + AHEAD, count):
                groups[h] = groups[h] - product[8 * h : 8 * h + 8, :]
    return groups


def matern(left, left_sq, right, right_sq):
    squared = left_sq + right_sq - 2.0 * stacked(left, right)
    scaled = root_three * jnp.sqrt(jnp.maximum(squared, 0.0))
    return (1.0 + scaled) * jnp.exp(-scaled)


def spread(jobs, slots):
    def fill(slot):
        for job in jobs[slot * len(jobs) // slots : (slot + 1) * len(jobs) // slots]:
            job()

    return fill


WIDTH = PB + RB
LAST = PB - RB


def factor_kernel(
    where_ref, blk_ref, col_ref, pan_ref, pnug_ref, nug_ref, len_ref,
    schur_ref, lower_ref,
    pts, cpts, nugs, sq_l, sq_r, sq_c, p_l, p_r, c_r, big, across, weights, u_ref, partial,
):
    r = where_ref[0]
    c = where_ref[1]
    inv = 1.0 / len_ref[...]
    pts[PB:, :] = blk_ref[...] * inv
    for rb in range(NC):
        nugs[:, rb * RB : (rb + 1) * RB] = pnug_ref[rb]
        for cc in range(NC):
            at = rb * RB + cc * SL
            both = pan_ref[cc, rb]
            pts[at : at + 8, :] = both[:, 0:F] * inv
            pts[at + 8 : at + SL, :] = both[:, F : 2 * F] * inv
    for rb in range(NR):
        both = col_ref[rb]
        cpts[rb * SL : rb * SL + 8, :] = both[:, 0:F] * inv
        cpts[rb * SL + 8 : rb * SL + SL, :] = both[:, F : 2 * F] * inv
    for i in range(NC + 1):
        at = i * RB
        block = pts[at : at + RB, :]
        turned = block.T
        sq_l[at : at + RB, :] = jnp.sum(block * block, axis=1, keepdims=True)
        sq_r[:, at : at + RB] = jnp.sum(turned * turned, axis=0, keepdims=True)
        p = parts(turned)
        p_l[:, at : at + RB] = left_stack(p)
        p_r[:, at : at + RB] = right_stack(p)
    for i in range(NC):
        at = i * RB
        turned = cpts[at : at + RB, :].T
        sq_c[:, at : at + RB] = jnp.sum(turned * turned, axis=0, keepdims=True)
        c_r[:, at : at + RB] = right_stack(parts(turned))

    eye = lax.broadcasted_iota(jnp.int32, (RB, RB), 0) == lax.broadcasted_iota(
        jnp.int32, (RB, RB), 1
    )
    low = lax.broadcasted_iota(jnp.int32, (RB, RB), 0) >= lax.broadcasted_iota(
        jnp.int32, (RB, RB), 1
    )
    sub = lax.broadcasted_iota(jnp.int32, (RB, 1), 0)

    def column_ids(start, width):
        n = start + lax.broadcasted_iota(jnp.int32, (1, width), 1)
        return lax.shift_right_logical(n, 4) * RB + c * SL + jnp.bitwise_and(n, SL - 1)

    def panel_job(i, lo, hi):
        def job():
            at = i * RB
            block = matern(
                p_l[:, at : at + RB], sq_l[at : at + RB, :], p_r[:, lo:hi], sq_r[:, lo:hi]
            )
            if lo == at:
                block = block + jnp.where(eye, nugs[0:1, at : at + RB], 0.0)
            if lo == PB:
                same = jnp.where(r == i, 1.0, 0.0)
                block = block + same * jnp.where(eye, nugs[0:1, at : at + RB], 0.0)
            big[at : at + RB, lo:hi] = block

        return job

    def across_job(i, lo, hi):
        def job():
            at = i * RB
            block = matern(
                p_l[:, at : at + RB], sq_l[at : at + RB, :], c_r[:, lo:hi], sq_c[:, lo:hi]
            )
            if lo < RB:
                nug_col = jnp.sum(
                    jnp.where(eye, nugs[0:1, at : at + RB], 0.0), axis=1, keepdims=True
                )
                block = block + jnp.where(at + sub == column_ids(lo, hi - lo), nug_col, 0.0)
            for q, part in enumerate(parts(block)[0:2]):
                across[q, at : at + RB, lo:hi] = part

        return job

    def keep(half, lo, hi, value):
        hi_p, mid_p, low_p = parts(value)
        u_ref[half, 0, :, lo:hi] = hi_p
        u_ref[half, 1, :, lo:hi] = mid_p
        u_ref[half, 2, :, lo:hi] = low_p

    def kept(half, lo, hi):
        return tuple(u_ref[half, q, :, lo:hi] for q in range(3))

    def row_job(k, left, lo, hi):
        def job():
            at = k * RB
            value = stacked(left, right_stack(parts(big[at : at + RB, lo:hi])), 1)
            big[at : at + RB, lo:hi] = value
            keep(k % 2, lo, hi, value)

        return job

    def update_job(k, i, lo, hi):
        def job():
            at = i * RB
            change = stacked(
                left_stack(kept(k % 2, at, at + RB)), right_stack(kept(k % 2, lo, hi))
            )
            if lo == k * RB:
                big[at : at + RB, lo:hi] = -change
            else:
                big[at : at + RB, lo:hi] = big[at : at + RB, lo:hi] - change

        return job

    def weight_job(j):
        def job():
            at = j * RB
            weights[at : at + RB, :] = stacked(
                left_short(parts(big[at:LAST, at : at + RB])),
                right_short(parts(big[at:LAST, PB:])),
            )

        return job

    def partial_job(lo, hi):
        def job():
            nug_own = jnp.sum(jnp.where(eye, nug_ref[...], 0.0), axis=1, keepdims=True)
            partial[:, lo:hi] = matern(
                p_l[:, PB:], sq_l[PB:, :], c_r[:, lo:hi], sq_c[:, lo:hi]
            ) + jnp.where(r * RB + sub == column_ids(lo, hi - lo), nug_own, 0.0)

        return job

    def lower_job(j):
        def job():
            at = j * RB
            lower_ref[:, at : at + RB] = big[at : at + RB, PB:].T

        return job

    def pieces(lo, hi, size=2 * RB):
        return [(x, min(hi, x + size)) for x in range(lo, hi, size)]

    panel_job(0, 0, RB)()
    jobs = []
    for i in range(NC):
        spans = pieces((i if i else 1) * RB, PB) if i == 0 else [(i * RB, (i + 1) * RB)]
        if i:
            spans = spans + pieces((i + 1) * RB, PB)
        jobs += [panel_job(i, lo, hi) for lo, hi in spans + [(PB, WIDTH)]]
    extra = {2: (0, 2), 3: (2, 9), 4: (9, 17), 5: (17, 25), 6: (25, 32)}
    slices = [(i, lo, hi) for i in range(NC) for lo, hi in pieces(0, PB)]
    square = big[0:RB, 0:RB]
    for k in range(NC):
        at = k * RB
        if k in extra:
            jobs += [across_job(*x) for x in slices[extra[k][0] : extra[k][1]]]
        if k == NC - 1:
            jobs += [lower_job(j) for j in range(NC - 1)]
            jobs += [partial_job(lo, hi) for lo, hi in pieces(0, PB)]
            jobs += [weight_job(j) for j in range(NC - 1)]
        groups = factor_block([square[h : h + 8, :] for h in range(0, RB, 8)], spread(jobs, RB))
        inverse = jnp.where(low, jnp.concatenate(groups, axis=0), 0.0)
        left = left_stack(parts(inverse), axis=1)
        nxt = at + RB
        if k < NC - 1:
            beside = stacked(left, right_stack(parts(big[at:nxt, nxt : nxt + RB])), 1)
            p = parts(beside)
            square = big[nxt : nxt + RB, nxt : nxt + RB] - stacked(left_stack(p), right_stack(p))
            keep(k % 2, nxt, nxt + RB, beside)
        big[at:nxt, at:nxt] = inverse
        keep(k % 2, at, nxt, inverse)
        jobs = [row_job(k, left, lo, hi) for lo, hi in pieces(0, at)]
        jobs += [row_job(k, left, lo, hi) for lo, hi in pieces(min(nxt + RB, PB), WIDTH)]
        for i in range(k + 1, NC):
            start = (i if i > k + 1 else i + 1) * RB
            spans = pieces(0, at) + [(at, nxt)] + pieces(start, WIDTH)
            jobs += [update_job(k, i, lo, hi) for lo, hi in spans]
    for job in jobs:
        job()
    lower_job(NC - 1)()
    change = stacked(
        left_short(parts(big[LAST:, 0:PB])), right_short(parts(big[LAST:, PB:]))
    )
    w_left = left_short(parts(jnp.concatenate([weights[0:LAST, :] + change[0:LAST], change[LAST:]], axis=0)))
    for lo, hi in pieces(0, PB):
        hi_p, mid_p = across[0, :, lo:hi], across[1, :, lo:hi]
        value = partial[:, lo:hi] - stacked(w_left, right_short((hi_p, mid_p)))
        for q in range(lo // RB, hi // RB):
            schur_ref[:, q, :] = value[:, q * RB - lo : (q + 1) * RB - lo]


def factor_and_update(where, blk, col, pan, pnug, nugget, lengthscale):
    vmem = pl.BlockSpec(memory_space=pltpu.VMEM)
    f32 = jnp.float32
    return pl.pallas_call(
        factor_kernel,
        out_shape=(
            jax.ShapeDtypeStruct((RB, NC, RB), f32),
            jax.ShapeDtypeStruct((RB, PB), f32),
        ),
        in_specs=[pl.BlockSpec(memory_space=pltpu.SMEM)] + [vmem] * 6,
        out_specs=(vmem, vmem),
        scratch_shapes=[
            pltpu.VMEM((WIDTH, F), f32),
            pltpu.VMEM((PB, F), f32),
            pltpu.VMEM((8, PB), f32),
            pltpu.VMEM((WIDTH, 1), f32),
            pltpu.VMEM((1, WIDTH), f32),
            pltpu.VMEM((1, PB), f32),
            pltpu.VMEM((6 * F, WIDTH), jnp.bfloat16),
            pltpu.VMEM((6 * F, WIDTH), jnp.bfloat16),
            pltpu.VMEM((6 * F, PB), jnp.bfloat16),
            pltpu.VMEM((PB, WIDTH), f32),
            pltpu.VMEM((2, PB, PB), jnp.bfloat16),
            pltpu.VMEM((PB, RB), f32),
            pltpu.VMEM((2, 3, RB, WIDTH), jnp.bfloat16),
            pltpu.VMEM((RB, PB), f32),
        ],
        compiler_params=pltpu.CompilerParams(vmem_limit_bytes=48 * 1024 * 1024),
        name="factor",
    )(where, blk, col, pan, pnug, nugget.reshape(1, RB), lengthscale.reshape(1, F))


def body(telemetry, target, counts, lengthscale, nugget):
    block_pts, col_packed, pan_packed, pnug = exchange(telemetry, target, counts, nugget)
    where = jnp.stack([lax.axis_index("row"), lax.axis_index("col")]).astype(jnp.int32)
    schur_tile, row_lower = factor_and_update(
        where, block_pts, col_packed, pan_packed, pnug, nugget, lengthscale
    )
    return (schur_tile.reshape(RB, 1, PB), row_lower)


def solution(mesh):
    in_specs = (P("col", "row", None), P("col", "row"), P("col", "row"), P(), P("row"))
    out_specs = (P("row", "col", None), P("row", None))
    return jax.shard_map(body, mesh=mesh, in_specs=in_specs, out_specs=out_specs, check_vma=False)
```

```python
import functools

import jax
import jax.numpy as jnp
from jax import lax
from jax.experimental import pallas as pl
from jax.experimental.pallas import tpu as pltpu
from jax.sharding import PartitionSpec as P

F = 64
PB = 1024
RB = 128
NR = 64
NC = 8
SL = 16
WIN = 16
SLOTS = 32
HI = lax.Precision.HIGHEST
MESH = pl.DeviceIdType.MESH

root_three = 1.7320508075688772


def hdot(a, b):
    return jnp.dot(a, b, precision=HI, preferred_element_type=jnp.float32)


def exchange_kernel(
    tel_ref, tgt_ref, cnt_ref, nug_ref, len_ref,
    blk_ref, col_ref, pan_ref, pnug_ref,
    out1, in1, comp, gath, mine, nugtile,
    s1, r1, s2, r2, s3, r3, s4, r4, s5, r5,
):
    r = lax.axis_index("row")
    c = lax.axis_index("col")

    def at_row(peer):
        return (peer, c)

    def at_col(peer):
        return (r, peer)

    barrier = pltpu.get_barrier_semaphore()

    def greet_row(i, carry):
        pl.semaphore_signal(
            barrier, inc=1, device_id=at_row(lax.rem(r + i, NR)), device_id_type=MESH
        )
        return carry

    def greet_col(i, carry):
        pl.semaphore_signal(
            barrier, inc=1, device_id=at_col(lax.rem(c + i, NC)), device_id_type=MESH
        )
        return carry

    lax.fori_loop(1, NR, greet_row, 0)
    lax.fori_loop(1, NC, greet_col, 0)

    tel = tel_ref[0] * (1.0 / len_ref[...])
    t_row = tgt_ref[...]
    sub = lax.broadcasted_iota(jnp.int32, (SLOTS, SLOTS), 0)
    lane = lax.broadcasted_iota(jnp.int32, (SLOTS, SLOTS), 1)
    t_mat = jnp.broadcast_to(t_row, (SLOTS, SLOTS))
    t_col = jnp.sum(jnp.where(sub == lane, t_mat, 0), axis=1, keepdims=True)
    zone_row = lax.shift_right_logical(t_row, 7)
    zone_col = lax.shift_right_logical(t_col, 7)
    filled = cnt_ref[...]
    earlier = (zone_col == zone_row) & (sub < filled) & (sub < lane)
    position = jnp.sum(earlier.astype(jnp.int32), axis=0, keepdims=True)
    offset = jnp.bitwise_and(r - zone_row + NR, NR - 1)
    used = (lane[0:1] < filled) & (position < 2) & (offset < WIN)
    slot = jnp.where(used, offset * 2 + position, -1)
    place = jnp.bitwise_and(t_row, RB - 1).astype(jnp.float32)
    dist = lax.broadcasted_iota(jnp.int32, (WIN, SLOTS), 0) * 2
    pick0 = dist == slot
    pick1 = dist + 1 == slot
    feat0 = hdot(pick0.astype(jnp.float32), tel)
    feat1 = hdot(pick1.astype(jnp.float32), tel)
    place0 = jnp.max(jnp.where(pick0, place, -1.0), axis=1, keepdims=True)
    place1 = jnp.max(jnp.where(pick1, place, -1.0), axis=1, keepdims=True)
    feats = jnp.concatenate([feat0, feat1], axis=1)
    lane_w = lax.broadcasted_iota(jnp.int32, (WIN, 128), 1)
    places = jnp.where(lane_w < F, place0, place1)
    tile_row = lax.broadcasted_iota(jnp.int32, (8, 128), 0)
    for d in range(WIN):
        out1[d] = jnp.where(
            tile_row == d % 8,
            feats[d : d + 1],
            jnp.where(tile_row == (d + 4) % 8, places[d : d + 1], 0.0),
        )
    in1[0] = out1[0]
    nugtile[...] = jnp.broadcast_to(nug_ref[...], (8, 128))

    pl.semaphore_wait(barrier, NR - 1 + NC - 1)

    def step1(d):
        return pltpu.make_async_remote_copy(
            src_ref=out1.at[d], dst_ref=in1.at[d], send_sem=s1, recv_sem=r1,
            device_id=at_row(jnp.bitwise_and(r - d + NR, NR - 1)), device_id_type=MESH,
        )

    def start1(d, carry):
        step1(d).start()
        return carry

    lax.fori_loop(1, WIN, start1, 0)

    def drain(ref, sem):
        pltpu.make_async_copy(ref, ref, sem).wait()

    def step5(i, slot_id):
        return pltpu.make_async_remote_copy(
            src_ref=nugtile, dst_ref=pnug_ref.at[slot_id], send_sem=s5, recv_sem=r5,
            device_id=at_row(jnp.bitwise_and(r + i, NR - 1)), device_id_type=MESH,
        )

    drain(in1.at[pl.ds(1, WIN - 1)], r1)
    for half in range(2):
        feat_rows = jnp.zeros((8, 128), jnp.float32)
        place_rows = jnp.zeros((8, 128), jnp.float32)
        for d in range(8):
            got = in1[8 * half + d]
            feat_rows = jnp.where(tile_row == d, got, feat_rows)
            place_rows = jnp.where(tile_row == (d + 4) % 8, got, place_rows)
        comp[8 * half : 8 * half + 8, :] = feat_rows
        comp[WIN + 8 * half : WIN + 8 * half + 8, :] = pltpu.roll(place_rows, 4, 0)

    def step2(i, slot_id):
        return pltpu.make_async_remote_copy(
            src_ref=comp, dst_ref=gath.at[slot_id], send_sem=s2, recv_sem=r2,
            device_id=at_col(jnp.bitwise_and(c + i, NC - 1)), device_id_type=MESH,
        )

    for i in range(1, NC):
        step2(i, c).start()
    gath[c] = comp[...]

    @pl.when(r < NC)
    def _():
        def start5(i, carry):
            step5(i, r).start()
            return carry

        lax.fori_loop(1, NR, start5, 0)
        pnug_ref[r] = nugtile[...]

    drain(gath.at[pl.ds(1, NC - 1)], r2)

    all_feats = gath[:, 0:WIN, :].reshape(NC * WIN, 128)
    all_places = gath[:, WIN : 2 * WIN, :].reshape(NC * WIN, 128)
    hi_p, mid_p, low_p = parts(all_feats)
    stack = jnp.concatenate([hi_p, mid_p, low_p], axis=0)

    def placed(first, count):
        spot = first + lax.broadcasted_iota(jnp.int32, (NC * WIN, count), 1)
        spot = spot.astype(jnp.float32)
        put0 = (all_places[:, 0:1] == spot).astype(jnp.bfloat16)
        put1 = (all_places[:, F : F + 1] == spot).astype(jnp.bfloat16)
        rows0 = stacked(jnp.concatenate([put0] * 3, axis=0), stack)
        rows1 = stacked(jnp.concatenate([put1] * 3, axis=0), stack)
        return rows0[:, 0:F] + rows1[:, F : 2 * F]

    group = placed(c * SL, SL)
    mine[:, 0:F] = group[0:8]
    mine[:, F : 2 * F] = group[8:SL]

    late = (r >= NC).astype(jnp.int32)

    def step3(i, slot_id):
        return pltpu.make_async_remote_copy(
            src_ref=mine, dst_ref=col_ref.at[slot_id], send_sem=s3, recv_sem=r3.at[late],
            device_id=at_row(jnp.bitwise_and(r + i, NR - 1)), device_id_type=MESH,
        )

    def start3(i, carry):
        step3(i, r).start()
        return carry

    lax.fori_loop(1, NR, start3, 0)
    col_ref[r] = mine[...]
    blk_ref[...] = placed(0, RB)

    @pl.when(r < NC)
    def _():
        drain(col_ref.at[pl.ds(0, NC - 1)], r3.at[0])

    @pl.when(r >= NC)
    def _():
        drain(col_ref.at[pl.ds(0, NC)], r3.at[0])

    def step4(i, slot_id):
        return pltpu.make_async_remote_copy(
            src_ref=col_ref.at[pl.ds(0, NC)], dst_ref=pan_ref.at[slot_id], send_sem=s4,
            recv_sem=r4,
            device_id=at_col(jnp.bitwise_and(c + i, NC - 1)), device_id_type=MESH,
        )

    for i in range(1, NC):
        step4(i, c).start()
    pan_ref[c] = col_ref[0:NC]

    @pl.when(r < NC)
    def _():
        drain(col_ref.at[pl.ds(NC, NR - NC)], r3.at[1])
        drain(pnug_ref.at[pl.ds(0, NC - 1)], r5)

    @pl.when(r >= NC)
    def _():
        drain(col_ref.at[pl.ds(NC, NR - NC - 1)], r3.at[1])
        drain(pnug_ref, r5)

    drain(in1.at[pl.ds(1, WIN - 1)], s1)
    drain(gath.at[pl.ds(1, NC - 1)], s2)
    drain(col_ref.at[pl.ds(1, NR - 1)], s3)
    drain(pan_ref.at[pl.ds(1, NC - 1)], r4)
    drain(pan_ref.at[pl.ds(1, NC - 1)], s4)

    @pl.when(r < NC)
    def _():
        drain(col_ref.at[pl.ds(1, NR - 1)], s5)


def exchange(telemetry, target, counts, nugget, lengthscale):
    dma = pltpu.SemaphoreType.DMA
    vmem = pl.BlockSpec(memory_space=pltpu.VMEM)
    f32 = jnp.float32
    return pl.pallas_call(
        exchange_kernel,
        out_shape=(
            jax.ShapeDtypeStruct((RB, F), f32),
            jax.ShapeDtypeStruct((NR, 8, 128), f32),
            jax.ShapeDtypeStruct((NC, NC, 8, 128), f32),
            jax.ShapeDtypeStruct((NC, 8, 128), f32),
        ),
        in_specs=[vmem] * 5,
        out_specs=(vmem,) * 4,
        scratch_shapes=[
            pltpu.VMEM((WIN, 8, 128), f32),
            pltpu.VMEM((WIN, 8, 128), f32),
            pltpu.VMEM((2 * WIN, 128), f32),
            pltpu.VMEM((NC, 2 * WIN, 128), f32),
            pltpu.VMEM((8, 128), f32),
            pltpu.VMEM((8, 128), f32),
            dma(()), dma(()), dma(()), dma(()), dma(()), dma((2,)),
            dma(()), dma(()), dma(()), dma(()),
        ],
        compiler_params=pltpu.CompilerParams(
            collective_id=0, has_side_effects=True, vmem_limit_bytes=32 * 1024 * 1024
        ),
        name="exchange",
    )(telemetry, target, counts, nugget.reshape(1, RB), lengthscale.reshape(1, F))


def sublanes(x, i):
    return jnp.broadcast_to(x[i : i + 1, :], (8, RB))


def lanes(x, j):
    return lax.gather(
        x,
        jnp.full((8, RB, 1), j, jnp.int32),
        lax.GatherDimensionNumbers(
            offset_dims=(), collapsed_slice_dims=(1,), start_index_map=(1,),
            operand_batching_dims=(0,), start_indices_batching_dims=(0,),
        ),
        slice_sizes=(1, 1),
        mode=lax.GatherScatterMode.PROMISE_IN_BOUNDS,
    )


def parts(x):
    f32 = jnp.float32
    hi = x.astype(jnp.bfloat16)
    rest = x - hi.astype(f32)
    mid = rest.astype(jnp.bfloat16)
    low = (rest - mid.astype(f32)).astype(jnp.bfloat16)
    return hi, mid, low


def left_stack(p, axis=0):
    hi, mid, low = p
    return jnp.concatenate([hi, hi, hi, mid, mid, low], axis=axis)


def right_stack(p):
    hi, mid, low = p
    return jnp.concatenate([hi, mid, low, hi, mid, hi], axis=0)


def left_short(p):
    return jnp.concatenate([p[0], p[0], p[1]], axis=0)


def right_short(p):
    return jnp.concatenate([p[0], p[1], p[0]], axis=0)


def stacked(left, right, over=0):
    return lax.dot_general(
        left, right, (((over,), (0,)), ((), ())), preferred_element_type=jnp.float32
    )


def gram(u):
    f32 = jnp.float32
    hi = u.astype(jnp.bfloat16).astype(f32)
    rest = u - hi
    mid = rest.astype(jnp.bfloat16).astype(f32)
    low = rest - mid
    left = jnp.concatenate([hi, hi, hi, mid, mid, low], axis=0).astype(jnp.bfloat16)
    right = jnp.concatenate([hi, mid, low, hi, mid, hi], axis=0).astype(jnp.bfloat16)
    return stacked(left, right)


AHEAD = 3


def factor_block(groups, fill):
    groups = list(groups)
    count = len(groups)
    sub = lax.broadcasted_iota(jnp.int32, (8, RB), 0)
    lane = lax.broadcasted_iota(jnp.int32, (8, RB), 1)
    for g in range(count):
        first = 8 * g
        near = list(range(g, min(count, g + AHEAD)))
        cols = {h: [lanes(groups[h], first + k) for k in range(8)] for h in near}
        in_panel = (lane >= first) & (lane < first + 8)
        one = (lane - first == sub).astype(jnp.float32)
        for h in range(g, count):
            groups[h] = jnp.where(in_panel, one if h == g else 0.0, groups[h])
        pivots = jnp.ones((8, RB), jnp.float32)
        small = [[sublanes(cols[g][k], i) if k >= i else None for k in range(8)] for i in range(8)]
        for i in range(8):
            fill(8 * g + i)
            inv = pl.reciprocal(small[i][i], approx=True)
            inv = inv * (2.0 - small[i][i] * inv)
            pivots = jnp.where(sub == i, small[i][i], pivots)
            row = sublanes(groups[g], i)
            for j in range(i + 1, 8):
                scale = small[i][j] * inv
                for k in range(j, 8):
                    small[j][k] = small[j][k] - scale * small[i][k]
            for h in near:
                step = cols[h][i] * inv
                if h == g:
                    step = jnp.where(sub > i, step, 0.0)
                for k in range(i + 1, 8):
                    cols[h][k] = cols[h][k] - step * small[i][k]
                if h != g or i < 7:
                    groups[h] = groups[h] - step * row
        done = groups[g] * lax.rsqrt(pivots)
        groups[g] = done
        if g + AHEAD < count:
            product = gram(done)
            for h in range(g + AHEAD, count):
                groups[h] = groups[h] - product[8 * h : 8 * h + 8, :]
    return groups


def matern(left, left_sq, right, right_sq):
    squared = jnp.maximum(left_sq + right_sq + stacked(left, right, 1), 1e-30)
    scaled = squared * lax.rsqrt(squared)
    return (1.0 + scaled) * jnp.exp(-scaled)


def spread(jobs, slots):
    def fill(slot):
        for job in jobs[slot * len(jobs) // slots : (slot + 1) * len(jobs) // slots]:
            job()

    return fill


WIDTH = PB + RB
LAST = PB - RB


def factor_kernel(
    where_ref, blk_ref, col_ref, pan_ref, pnug_ref, nug_ref,
    schur_ref, lower_ref,
    pts, cpts, nugs, sq_l, sq_r, sq_c, p_l, p_r, c_r, big, across, weights, u_ref, partial, l_ref,
):
    r = where_ref[0]
    c = where_ref[1]

    def prepare(i):
        def job():
            at = i * RB
            if i == NC:
                block = blk_ref[...]
            else:
                nugs[:, at : at + RB] = pnug_ref[i]
                for cc in range(NC):
                    both = pan_ref[cc, i]
                    pts[at + cc * SL : at + cc * SL + 8, :] = both[:, 0:F]
                    pts[at + cc * SL + 8 : at + cc * SL + SL, :] = both[:, F : 2 * F]
                block = pts[at : at + RB, :]
            turned = block.T
            sq_l[at : at + RB, :] = 3.0 * jnp.sum(block * block, axis=1, keepdims=True)
            sq_r[:, at : at + RB] = 3.0 * jnp.sum(turned * turned, axis=0, keepdims=True)
            wide = left_stack(tuple(q.astype(jnp.float32) for q in parts(-6.0 * turned)))
            p_l[at : at + RB, :] = wide.T.astype(jnp.bfloat16)
            p_r[:, at : at + RB] = right_stack(parts(turned))

        return job

    def prepare_columns(i):
        def job():
            at = i * RB
            for q in range(NC):
                both = col_ref[i * NC + q]
                cpts[at + q * SL : at + q * SL + 8, :] = both[:, 0:F]
                cpts[at + q * SL + 8 : at + q * SL + SL, :] = both[:, F : 2 * F]
            turned = cpts[at : at + RB, :].T
            sq_c[:, at : at + RB] = 3.0 * jnp.sum(turned * turned, axis=0, keepdims=True)
            c_r[:, at : at + RB] = right_stack(parts(turned))

        return job

    eye = lax.broadcasted_iota(jnp.int32, (RB, RB), 0) == lax.broadcasted_iota(
        jnp.int32, (RB, RB), 1
    )
    low = lax.broadcasted_iota(jnp.int32, (RB, RB), 0) >= lax.broadcasted_iota(
        jnp.int32, (RB, RB), 1
    )
    sub = lax.broadcasted_iota(jnp.int32, (RB, 1), 0)

    def column_ids(start, width):
        n = start + lax.broadcasted_iota(jnp.int32, (1, width), 1)
        return lax.shift_right_logical(n, 4) * RB + c * SL + jnp.bitwise_and(n, SL - 1)

    def panel_job(i, lo, hi):
        def job():
            at = i * RB
            block = matern(
                p_l[at : at + RB, :], sq_l[at : at + RB, :], p_r[:, lo:hi], sq_r[:, lo:hi]
            )
            if lo == at:
                block = block + jnp.where(eye, nugs[0:1, at : at + RB], 0.0)
            if lo == PB:
                same = jnp.where(r == i, 1.0, 0.0)
                block = block + same * jnp.where(eye, nugs[0:1, at : at + RB], 0.0)
            big[at : at + RB, lo:hi] = block

        return job

    def across_job(i, lo, hi):
        def job():
            at = i * RB
            block = matern(
                p_l[at : at + RB, :], sq_l[at : at + RB, :], c_r[:, lo:hi], sq_c[:, lo:hi]
            )
            if lo < RB:
                nug_col = jnp.sum(
                    jnp.where(eye, nugs[0:1, at : at + RB], 0.0), axis=1, keepdims=True
                )
                block = block + jnp.where(at + sub == column_ids(lo, hi - lo), nug_col, 0.0)
            for q, part in enumerate(parts(block)[0:2]):
                across[q, at : at + RB, lo:hi] = part

        return job

    def keep(k, lo, hi, value):
        half = k % 2
        for x in range(max(lo, (k + 1) * RB), min(hi, PB), RB):
            for q, part in enumerate(parts(value[:, x - lo : x - lo + RB].T)):
                l_ref[half, q, x : x + RB, :] = part
        hi_p, mid_p, low_p = parts(value)
        u_ref[half, 0, :, lo:hi] = hi_p
        u_ref[half, 1, :, lo:hi] = mid_p
        u_ref[half, 2, :, lo:hi] = low_p

    def kept(half, lo, hi):
        return tuple(u_ref[half, q, :, lo:hi] for q in range(3))

    def row_job(k, left, lo, hi):
        def job():
            at = k * RB
            value = stacked(left, right_stack(parts(big[at : at + RB, lo:hi])), 1)
            big[at : at + RB, lo:hi] = value
            keep(k, lo, hi, value)

        return job

    def update_job(k, i, lo, hi):
        def job():
            at = i * RB
            change = stacked(
                left_stack(tuple(l_ref[k % 2, q, at : at + RB, :] for q in range(3)), axis=1),
                right_stack(kept(k % 2, lo, hi)),
                1,
            )
            if lo == k * RB:
                big[at : at + RB, lo:hi] = -change
            else:
                big[at : at + RB, lo:hi] = big[at : at + RB, lo:hi] - change

        return job

    def weight_job(j):
        def job():
            at = j * RB
            weights[at : at + RB, :] = stacked(
                left_short(parts(big[at:LAST, at : at + RB])),
                right_short(parts(big[at:LAST, PB:])),
            )

        return job

    def partial_job(lo, hi):
        def job():
            nug_own = jnp.sum(jnp.where(eye, nug_ref[...], 0.0), axis=1, keepdims=True)
            partial[:, lo:hi] = matern(
                p_l[PB:, :], sq_l[PB:, :], c_r[:, lo:hi], sq_c[:, lo:hi]
            ) + jnp.where(r * RB + sub == column_ids(lo, hi - lo), nug_own, 0.0)

        return job

    def lower_job(j):
        def job():
            at = j * RB
            lower_ref[:, at : at + RB] = big[at : at + RB, PB:].T

        return job

    def pieces(lo, hi, size=2 * RB):
        return [(x, min(hi, x + size)) for x in range(lo, hi, size)]

    prepare(0)()
    panel_job(0, 0, RB)()
    jobs = [prepare(i) for i in range(1, NC + 1)]
    for i in range(NC):
        spans = pieces((i if i else 1) * RB, PB) if i == 0 else [(i * RB, (i + 1) * RB)]
        if i:
            spans = spans + pieces((i + 1) * RB, PB)
        jobs += [panel_job(i, lo, hi) for lo, hi in spans + [(PB, WIDTH)]]
    extra = {2: (0, 2), 3: (2, 9), 4: (9, 17), 5: (17, 25), 6: (25, 32)}
    slices = [(i, lo, hi) for i in range(NC) for lo, hi in pieces(0, PB)]
    square = big[0:RB, 0:RB]
    for k in range(NC):
        at = k * RB
        if k == 2:
            jobs = [prepare_columns(i) for i in range(NC)] + jobs
        if k in extra:
            jobs += [across_job(*x) for x in slices[extra[k][0] : extra[k][1]]]
        if k == NC - 1:
            jobs += [lower_job(j) for j in range(NC - 1)]
            jobs += [partial_job(lo, hi) for lo, hi in pieces(0, PB)]
            jobs += [weight_job(j) for j in range(NC - 1)]
        groups = factor_block([square[h : h + 8, :] for h in range(0, RB, 8)], spread(jobs, RB))
        inverse = jnp.where(low, jnp.concatenate(groups, axis=0), 0.0)
        left = left_stack(parts(inverse), axis=1)
        nxt = at + RB
        if k < NC - 1:
            beside = stacked(left, right_stack(parts(big[at:nxt, nxt : nxt + RB])), 1)
            p = parts(beside)
            square = big[nxt : nxt + RB, nxt : nxt + RB] - stacked(left_stack(p), right_stack(p))
            keep(k, nxt, nxt + RB, beside)
        big[at:nxt, at:nxt] = inverse
        keep(k, at, nxt, inverse)
        jobs = [row_job(k, left, lo, hi) for lo, hi in pieces(0, at)]
        jobs += [row_job(k, left, lo, hi) for lo, hi in pieces(min(nxt + RB, PB), WIDTH)]
        for i in range(k + 1, NC):
            start = (i if i > k + 1 else i + 1) * RB
            spans = pieces(0, at) + [(at, nxt)] + pieces(start, WIDTH)
            jobs += [update_job(k, i, lo, hi) for lo, hi in spans]
    for job in jobs:
        job()
    lower_job(NC - 1)()
    change = stacked(
        left_short(parts(big[LAST:, 0:PB])), right_short(parts(big[LAST:, PB:]))
    )
    w_left = left_short(parts(jnp.concatenate([weights[0:LAST, :] + change[0:LAST], change[LAST:]], axis=0)))
    for lo, hi in pieces(0, PB):
        hi_p, mid_p = across[0, :, lo:hi], across[1, :, lo:hi]
        value = partial[:, lo:hi] - stacked(w_left, right_short((hi_p, mid_p)))
        for q in range(lo // RB, hi // RB):
            schur_ref[:, q, :] = value[:, q * RB - lo : (q + 1) * RB - lo]


def factor_and_update(where, blk, col, pan, pnug, nugget):
    vmem = pl.BlockSpec(memory_space=pltpu.VMEM)
    f32 = jnp.float32
    return pl.pallas_call(
        factor_kernel,
        out_shape=(
            jax.ShapeDtypeStruct((RB, NC, RB), f32),
            jax.ShapeDtypeStruct((RB, PB), f32),
        ),
        in_specs=[pl.BlockSpec(memory_space=pltpu.SMEM)] + [vmem] * 5,
        out_specs=(vmem, vmem),
        scratch_shapes=[
            pltpu.VMEM((WIDTH, F), f32),
            pltpu.VMEM((PB, F), f32),
            pltpu.VMEM((8, PB), f32),
            pltpu.VMEM((WIDTH, 1), f32),
            pltpu.VMEM((1, WIDTH), f32),
            pltpu.VMEM((1, PB), f32),
            pltpu.VMEM((WIDTH, 6 * F), jnp.bfloat16),
            pltpu.VMEM((6 * F, WIDTH), jnp.bfloat16),
            pltpu.VMEM((6 * F, PB), jnp.bfloat16),
            pltpu.VMEM((PB, WIDTH), f32),
            pltpu.VMEM((2, PB, PB), jnp.bfloat16),
            pltpu.VMEM((PB, RB), f32),
            pltpu.VMEM((2, 3, RB, WIDTH), jnp.bfloat16),
            pltpu.VMEM((RB, PB), f32),
            pltpu.VMEM((2, 3, PB, RB), jnp.bfloat16),
        ],
        compiler_params=pltpu.CompilerParams(vmem_limit_bytes=48 * 1024 * 1024),
        name="factor",
    )(where, blk, col, pan, pnug, nugget.reshape(1, RB))


def body(telemetry, target, counts, lengthscale, nugget):
    block_pts, col_packed, pan_packed, pnug = exchange(
        telemetry, target, counts, nugget, lengthscale
    )
    where = jnp.stack([lax.axis_index("row"), lax.axis_index("col")]).astype(jnp.int32)
    schur_tile, row_lower = factor_and_update(
        where, block_pts, col_packed, pan_packed, pnug, nugget
    )
    return (schur_tile.reshape(RB, 1, PB), row_lower)


def solution(mesh):
    in_specs = (P("col", "row", None), P("col", "row"), P("col", "row"), P(), P("row"))
    out_specs = (P("row", "col", None), P("row", None))
    return jax.shard_map(body, mesh=mesh, in_specs=in_specs, out_specs=out_specs, check_vma=False)
```
